1024 devices in a mesh: ctx: 16 (over z_lo), exp: 64 (over x, z_hi, y, core).
Axes of the slice: x: 4, y: 4, z: 32 (z_hi: 2, z_lo: 16; z = z_hi * 16 + z_lo), core: 2. Of those that a mesh axis runs over, the one named last changes fastest.
Arguments:
- queries: bfloat16 [2048, 8192], P('ctx', 'exp'), may hold values from -8 to 8
- keys_values: bfloat16 [2048, 1024], P('ctx'), may hold values from -8 to 8
- residual: bfloat16 [2048, 4096], P(('ctx', 'exp')), may hold values from -1.1953125 to 1.1953125
- norm_gain: float32 [4096], replicated, may hold values from 0.5 to 1.5
- out_weight: bfloat16 [8192, 4096], P('exp'), may hold values from -0.0625 to 0.0625
- expert_ids: int32 [2048, 8], P('exp'), may hold values from 0 to 63, all different within a row; in each aligned block of 32 rows (0 to 31, 32 to 63, ...) at most 5 rows name the same one
- gate_values: float32 [2048, 8], P('exp'), may hold values from 0.1 to 1
- gate_up_weight: bfloat16 [64, 4096, 3072], P('exp', 'ctx'), may hold values from -0.09375 to 0.09375
- down_weight: bfloat16 [64, 1536, 4096], P('exp', None, 'ctx'), may hold values from -0.15625 to 0.15625
Outputs:
- layer_out: bfloat16 [2048, 4096], P('exp', 'ctx')
The draws below stay inside these ranges and needn't reach their ends.
Inputs may be any that keep to these rules, and one draw needn't show every extreme that they name: `expert_ids`: in the 32 rows of one routing group no expert is chosen more than 5 times.
All inputs are finite; a program needn't handle non-finite values.
Results may differ from the reference program's by a relative error of at most 0.033.
Values may be sent and summed in bfloat16 or wider, within the bound.
No kernel may reach another device: no remote copies, remote signals or barrier semaphores. Data moves between devices by JAX's collectives and lax.ppermute only.
A program may use at most 32 MiB of HBM per device.

```python
import math
import jax
import jax.numpy as jnp
import numpy as np
from jax import lax

D = 4096
HEADS = 64
KV_HEADS = 4
HD = 128
FFE = 1536
TOPK = 8
EXPERTS = 64
TOKENS = 2048
SHARE = 2
COL_TOK = 32
CAP = 5
FEAT_DEV = 256
N_CTX = 16
N_EXP = 64


def draw_queries(key, part):
    key = jax.random.fold_in(key, 11)
    values = jnp.clip(1.5 * jax.random.normal(key, (TOKENS, HEADS * HD), jnp.float32), -6.0, 6.0)
    return values.astype(jnp.bfloat16)


def draw_keys_values(key, part):
    key = jax.random.fold_in(key, 12)
    key_first, key_second = jax.random.split(key)
    keys = jnp.clip(1.5 * jax.random.normal(key_first, (TOKENS, KV_HEADS * HD), jnp.float32), -6.0, 6.0)
    values = jnp.clip(jax.random.normal(key_second, (TOKENS, KV_HEADS * HD), jnp.float32), -4.0, 4.0)
    return jnp.concatenate([keys, values], axis=1).astype(jnp.bfloat16)


def shard_levels(key, extent, cuts, low, top_value):
    def one(axis_at, parts):
        draws = jax.random.uniform(jax.random.fold_in(jax.random.fold_in(key, 6), axis_at), (parts,), jnp.float32, low / len(cuts), top_value / len(cuts))
        return jnp.repeat(jnp.exp(draws), extent[axis_at] // parts).reshape((-1,) + (1,) * (len(extent) - axis_at - 1))

    gain = one(*cuts[0])
    for cut in cuts[1:]:
        gain = gain * one(*cut)
    return gain


def assign_block(own_key, own, number, rows, amount, top, reach, lean):
    sequence = jax.random.permutation(own_key, amount)
    packed, ordinary = shares(amount, rows * top, reach, lean, True), shares(amount, rows * top, reach, lean, False)
    places = jnp.arange(amount)

    def named(lengths, turn):
        used = int((lengths > 0).sum())
        fixed = max(1, used // 4)
        passed = fixed + (places - fixed + turn * (used - fixed)) % max(1, amount - fixed)
        return jnp.zeros((amount,), jnp.int32).at[sequence[jnp.where(places < fixed, places, passed)]].set(jnp.asarray(lengths, jnp.int32))

    lengths = jnp.where(number % 4 == 0, named(packed, number // 4), named(ordinary, number - number // 4 - 1))
    mixed = jax.random.permutation(jax.random.fold_in(own, 3), amount)
    giver, receiver = mixed[0:amount // 2 * 2:2], mixed[1:amount // 2 * 2:2]
    slack = jnp.minimum(lengths[giver] - 1, reach - lengths[receiver]) // 2
    slack = jnp.where((giver == sequence[0]) | (receiver == sequence[0]) | (lengths[receiver] == 0), 0, jnp.maximum(slack, 0))
    passed = jax.random.randint(jax.random.fold_in(own, 4), (amount // 2,), 0, 1 << 20) % (slack + 1)
    lengths = lengths.at[giver].add(-passed).at[receiver].add(passed)
    items = jnp.searchsorted(jnp.cumsum(lengths), jnp.arange(rows * top), side="right").astype(jnp.int32)
    grid = items.reshape(top, rows).T
    grid = grid[jax.random.permutation(jax.random.fold_in(own, 1), rows)]
    turn = jax.random.randint(jax.random.fold_in(own, 2), (rows, 1), 0, top)
    return jnp.take_along_axis(grid, (jnp.arange(top)[None, :] + turn) % top, axis=1)


def shares(count, total, limit, lean, full):
    portions = [(1 << 20) // math.isqrt(grade ** lean) + 1 for grade in range(1, count + 1)]
    largest = limit if full else min(limit, max(-(-total // count), total * portions[0] // sum(portions)))
    least = 1 if total - largest >= count - 1 else 0
    holding, spare = [largest] + [least] * (count - 1), total - largest - least * (count - 1)
    while spare > 0:
        movable = [i for i in range(1, count) if holding[i] < largest] or [i for i in range(1, count) if holding[i] < limit]
        pool, remaining = sum([portions[i] for i in movable]), spare
        for i in movable:
            addition = min(limit - holding[i], max(1, remaining * portions[i] // pool), spare)
            holding[i] = holding[i] + addition
            spare = spare - addition
    return np.array(holding)


def centred(stream_key, dims, deviation, bound, cuts=(), kind=jnp.bfloat16):
    values = jax.random.normal(stream_key, dims, jnp.float32) * deviation
    if len(cuts) > 0:
        values = shard_levels(stream_key, dims, cuts, -0.22, 0.18) * values
    return jnp.clip(values, min=-bound, max=bound).astype(kind)


def setup_inputs(seed: int = 0) -> dict:
    key_of = jax.random.split(jax.random.key(seed), 10)
    queries = draw_queries(jax.random.fold_in(key_of[9], 71), 0)
    keys_values = draw_keys_values(jax.random.fold_in(key_of[9], 71), 0)
    residual = centred(key_of[2], (TOKENS, D), 0.2, 1.1953125, ((0, 1024),))
    norm_gain = jnp.clip(1.0 + 0.1 * jax.random.normal(key_of[3], (D,), jnp.float32), 0.5, 1.5)
    out_weight = centred(key_of[4], (HEADS * HD, D), (HEADS * HD) ** -0.5, 0.0625, ((0, 64),))
    expert_ids_keys = jax.random.split(jax.random.fold_in(key_of[5], 1), TOKENS // COL_TOK)
    expert_ids_turns = jax.random.permutation(jax.random.fold_in(key_of[5], 3), TOKENS // COL_TOK)
    expert_ids = jax.vmap(lambda own, number: assign_block(jax.random.fold_in(key_of[5], 2), own, number, COL_TOK, EXPERTS, TOPK, CAP, 2))(expert_ids_keys, expert_ids_turns).reshape((TOKENS, TOPK))
    gate_values = jnp.clip(0.1 + 0.9 * jax.random.uniform(key_of[6], (TOKENS, TOPK), jnp.float32) ** shard_levels(key_of[6], (TOKENS, TOPK), ((0, 64),), -0.2, 0.2), 0.1, 1.0)
    gate_up_weight = centred(key_of[7], (EXPERTS, D, 2 * FFE), D ** -0.5, 0.09375, ((0, 64), (1, 16)))
    down_weight = centred(key_of[8], (EXPERTS, FFE, D), FFE ** -0.5, 0.15625, ((0, 64), (2, 16)))
    return {"queries": queries, "keys_values": keys_values, "residual": residual, "norm_gain": norm_gain, "out_weight": out_weight, "expert_ids": expert_ids, "gate_values": gate_values, "gate_up_weight": gate_up_weight, "down_weight": down_weight}


masked_score = -1e+30

def to_columns(array):
    return array.reshape(N_CTX, N_EXP, SHARE, -1).transpose(1, 0, 2, 3).reshape(TOKENS, -1)

def reference(queries, keys_values, residual, norm_gain, out_weight, expert_ids, gate_values, gate_up_weight, down_weight):
    group_size = HEADS // KV_HEADS
    positions = jnp.arange(TOKENS, dtype=jnp.int32)
    allowed = positions[None, :] <= positions[:, None]

    def one_head(head):
        kv_index = head // group_size
        query_part = lax.dynamic_slice_in_dim(queries, head * HD, HD, 1)
        key_part = lax.dynamic_slice_in_dim(keys_values, kv_index * HD, HD, 1)
        value_part = lax.dynamic_slice_in_dim(keys_values, KV_HEADS * HD + kv_index * HD, HD, 1)
        scores = jnp.dot(query_part, key_part.T, preferred_element_type=jnp.float32) * HD ** (-0.5)
        scores = jnp.where(allowed, scores, masked_score)
        top_score = lax.optimization_barrier(jnp.max(scores, axis=-1, keepdims=True))
        weights = jnp.where(allowed, jnp.exp(scores - top_score), 0.0)
        total = lax.optimization_barrier(jnp.sum(weights, axis=-1, keepdims=True))
        summed = jnp.dot(weights.astype(jnp.bfloat16), value_part, preferred_element_type=jnp.float32)
        return (summed / total).astype(jnp.bfloat16)
    heads_out = lax.map(one_head, jnp.arange(HEADS, dtype=jnp.int32))
    attended = heads_out.transpose(1, 0, 2).reshape(TOKENS, HEADS * HD)
    attn_rows = jnp.dot(attended, out_weight, preferred_element_type=jnp.float32)
    hidden_state = (residual.astype(jnp.float32) + attn_rows).astype(jnp.bfloat16)
    widened = hidden_state.astype(jnp.float32)
    mean_square = lax.optimization_barrier(jnp.mean(widened * widened, axis=-1, keepdims=True))
    normed = (widened * lax.rsqrt(mean_square + 1e-06) * norm_gain).astype(jnp.bfloat16)
    hidden_cols = to_columns(hidden_state)
    normed_cols = to_columns(normed)
    groups = TOKENS // COL_TOK
    id_blocks = expert_ids.reshape(groups, COL_TOK, TOPK)
    gate_blocks = gate_values.reshape(groups, COL_TOK, TOPK)
    picked = id_blocks[:, :, :, None] == jnp.arange(EXPERTS, dtype=jnp.int32)[None, None, None, :]
    chosen = lax.optimization_barrier(jnp.sum(picked.astype(jnp.int32), axis=2))
    slot_index = jnp.cumsum(chosen, axis=1, dtype=jnp.int32) - chosen
    gate_table = lax.optimization_barrier(jnp.sum(jnp.where(picked, gate_blocks[:, :, :, None], 0.0), axis=2))
    placed = (chosen[:, :, :, None] > 0) & (slot_index[:, :, :, None] == jnp.arange(CAP, dtype=jnp.int32)[None, None, None, :])
    blocks_in = normed_cols.reshape(groups, COL_TOK, D).astype(jnp.float32)

    def one_expert(expert):
        selector = lax.dynamic_index_in_dim(placed, expert, 2, keepdims=False).astype(jnp.float32)
        buffer = jnp.einsum('bts,btd->bsd', selector, blocks_in).astype(jnp.bfloat16)
        buffer = buffer.reshape(groups * CAP, N_CTX, FEAT_DEV).astype(jnp.float32)
        weight_in = lax.dynamic_index_in_dim(gate_up_weight, expert, 0, keepdims=False)
        weight_in = weight_in.reshape(N_CTX, FEAT_DEV, 2 * FFE).astype(jnp.float32)
        partial_sums = jnp.einsum('scd,cdf->scf', buffer, weight_in)
        rounded = lax.optimization_barrier(partial_sums.astype(jnp.bfloat16))
        gate_up = lax.optimization_barrier(jnp.sum(rounded.astype(jnp.float32), axis=1))
        activated = (jax.nn.silu(gate_up[:, :FFE]) * gate_up[:, FFE:]).astype(jnp.bfloat16)
        weight_out = lax.dynamic_index_in_dim(down_weight, expert, 0, keepdims=False)
        result = jnp.dot(activated, weight_out, preferred_element_type=jnp.float32).astype(jnp.bfloat16)
        return result.reshape(groups, CAP, D)
    expert_out = lax.map(one_expert, jnp.arange(EXPERTS, dtype=jnp.int32))
    combine = gate_table[:, :, :, None] * placed.astype(jnp.float32)
    mixed_rows = jnp.einsum('btxs,xbsd->btd', combine, expert_out.astype(jnp.float32), precision=lax.Precision.HIGHEST)
    return (hidden_cols.astype(jnp.float32) + mixed_rows.reshape(TOKENS, D)).astype(jnp.bfloat16)
```

```python
import jax
import jax.numpy as jnp
from jax import lax
from jax.sharding import Mesh, PartitionSpec as P

HD = 128
KV_HEADS = 4
CAP = 5

NP, NQ = 4, 4
NX, NZ, NY, NC = 4, 2, 4, 2

CTX = ("p", "q")
EXP = ("x", "zh", "y", "core")
PLANE = ("x", "y", "core")
NPLANE = NX * NY * NC
NCTX = NP * NQ

masked_score = -1e30
f32 = jnp.float32
bf16 = jnp.bfloat16


def swap(array, axes):
    return lax.all_to_all(array, axes, split_axis=0, concat_axis=0, tiled=True)


def share(block, axes, count):
    return swap(jnp.broadcast_to(block[None], (count,) + block.shape), axes)


def dot(a, b):
    return jnp.dot(a, b, preferred_element_type=f32)


def neighbour_blocks(blocks, q_index):
    received = []
    for k in range(NQ):
        mine = blocks(jnp.bitwise_xor(q_index, k))
        if k > 0:
            mine = lax.ppermute(mine, "q", [(i, i ^ k) for i in range(NQ)])
        received.append(mine)
    return received


def gather_keys_values(keys_values, x_index):
    rows = keys_values.shape[0]
    pieces = NY * NC
    height = rows // pieces
    piece = lax.axis_index(("y", "core"))
    key_piece = lax.dynamic_slice(keys_values, (piece * height, x_index * HD), (height, HD))
    value_piece = lax.dynamic_slice(
        keys_values, (piece * height, (KV_HEADS + x_index) * HD), (height, HD)
    )
    own = jnp.concatenate([key_piece, value_piece], axis=1)
    column = share(own, CTX, NCTX)
    segment = share(column, ("y", "core"), pieces).reshape(NCTX * rows, 2 * HD)
    number = jnp.arange(NCTX * rows, dtype=jnp.int32)
    key_pos = (
        (number % (NCTX * height)) // height * rows
        + number // (NCTX * height) * height
        + number % height
    )
    return segment[:, :HD], segment[:, HD:], key_pos


def attend(queries, key_part, value_part, key_pos, ctx_index):
    rows = queries.shape[0]
    query_pos = ctx_index * rows + jnp.arange(rows, dtype=jnp.int32)
    scores = (
        jnp.einsum("qd,kd->qk", queries, key_part, preferred_element_type=f32) * HD ** (-0.5)
    )
    allowed = key_pos[None, :] <= query_pos[:, None]
    scores = jnp.where(allowed, scores, masked_score)
    top = jnp.max(scores, axis=-1, keepdims=True)
    weights = jnp.where(allowed, jnp.exp(scores - top), 0.0)
    total = jnp.sum(weights, axis=-1, keepdims=True)
    return (dot(weights.astype(bf16), value_part) / total).astype(bf16)


def shards(
    queries,
    keys_values,
    residual,
    norm_gain,
    out_weight,
    expert_ids,
    gate_values,
    gate_up_weight,
    down_weight,
):
    p_index = lax.axis_index("p")
    q_index = lax.axis_index("q")
    x_index = lax.axis_index("x")
    zh_index = lax.axis_index("zh")
    ctx_index = lax.axis_index(CTX)
    gate_up_weight = gate_up_weight[0]
    down_weight = down_weight[0]
    feat = down_weight.shape[1]
    units = down_weight.shape[0] // NQ
    width = NQ * feat
    model = NP * width

    def gate_up_block(target):
        gate = lax.dynamic_slice(gate_up_weight, (0, target * units), (feat, units))
        up = lax.dynamic_slice(gate_up_weight, (0, (NQ + target) * units), (feat, units))
        return jnp.concatenate([gate, up], axis=1)

    def down_block(target):
        return lax.dynamic_slice(down_weight, (target * units, 0), (units, feat))

    flip = [(i, NZ - 1 - i) for i in range(NZ)]
    other_ids = lax.ppermute(expert_ids, "zh", flip)
    other_gates = lax.ppermute(gate_values, "zh", flip)

    key_part, value_part, key_pos = gather_keys_values(keys_values, x_index)
    weight_in = neighbour_blocks(gate_up_block, q_index)
    weight_out = neighbour_blocks(down_block, q_index)
    attended = attend(queries, key_part, value_part, key_pos, ctx_index)

    share_rows = attended.shape[0] // (NPLANE * NZ)
    attended = (
        attended.reshape(NX, NZ, NY, NC, share_rows, HD)
        .transpose(0, 2, 3, 1, 4, 5)
        .reshape(-1, HD)
    )
    partial = dot(attended, out_weight).astype(bf16).reshape(NPLANE, NZ * share_rows, model)
    partial = jnp.sum(swap(partial, PLANE).astype(f32), axis=0).reshape(NZ, share_rows, model)
    own_group = jnp.arange(NZ)[:, None, None] == zh_index
    partial = partial + jnp.where(own_group, residual.astype(f32)[None], 0.0)
    outgoing = (
        partial.astype(bf16)
        .reshape(NZ * share_rows, NP, 1, 1, width)
        .transpose(1, 2, 3, 0, 4)
    )
    outgoing = jnp.broadcast_to(outgoing, (NP, NQ, NZ, NZ * share_rows, width)).reshape(
        NCTX * NZ, NZ * share_rows, width
    )
    arrived = swap(outgoing, CTX + ("zh",)).reshape(NCTX, NZ, NZ * share_rows, width)
    hidden = jnp.sum(arrived.astype(f32), axis=1).astype(bf16).reshape(-1, width)

    hidden = jnp.concatenate(
        [
            lax.dynamic_slice_in_dim(hidden, jnp.bitwise_xor(q_index, k) * feat, feat, 1)
            for k in range(NQ)
        ],
        axis=1,
    )
    gain = jnp.concatenate(
        [
            lax.dynamic_slice_in_dim(
                norm_gain, (p_index * NQ + jnp.bitwise_xor(q_index, k)) * feat, feat, 0
            )
            for k in range(NQ)
        ]
    )

    token_count = expert_ids.shape[0]
    first = zh_index == 0
    ids = jnp.stack(
        [jnp.where(first, expert_ids, other_ids), jnp.where(first, other_ids, expert_ids)]
    )
    gates = jnp.stack(
        [jnp.where(first, gate_values, other_gates), jnp.where(first, other_gates, gate_values)]
    )
    number = jnp.arange(NPLANE, dtype=jnp.int32)
    experts = (number // (NY * NC) * NZ + zh_index) * (NY * NC) + number % (NY * NC)
    picked = ids[..., None] == experts
    chosen = jnp.sum(picked.astype(jnp.int32), axis=2)
    slot_index = jnp.cumsum(chosen, axis=1, dtype=jnp.int32) - chosen
    gate_table = jnp.sum(jnp.where(picked, gates[..., None], 0.0), axis=2)
    placed = (chosen[..., None] > 0) & (
        slot_index[..., None] == jnp.arange(CAP, dtype=jnp.int32)
    )
    same = jnp.eye(NZ, dtype=bool)[:, :, None, None, None]
    spread = (placed[:, None] & same).astype(f32)
    spread_gate = spread * gate_table[:, None, :, :, None]
    slots = NZ * CAP
    total_slots = NPLANE * slots
    selector = (
        spread.astype(bf16)
        .reshape(NZ, NZ, NCTX, share_rows, NPLANE, CAP)
        .transpose(4, 1, 5, 2, 0, 3)
        .reshape(total_slots, NZ * token_count)
    )
    combine = spread_gate.transpose(0, 2, 3, 1, 4).reshape(NZ * token_count, total_slots)

    buckets = dot(selector, hidden).astype(bf16).reshape(NPLANE, slots, width)
    buffer = swap(buckets, PLANE).reshape(total_slots, width).astype(f32)
    squares = jnp.sum(buffer * buffer, axis=1)
    scaled = (buffer * gain).astype(bf16)
    gate_up = dot(scaled[:, :feat], weight_in[0])
    for k in range(1, NQ):
        gate_up = gate_up + dot(scaled[:, k * feat : (k + 1) * feat], weight_in[k])

    rows = total_slots // NP
    chunks = 2 * units // HD
    high = squares.astype(bf16)
    low = (squares - high.astype(f32)).astype(bf16)
    pair = jnp.stack([high.reshape(NP, rows), low.reshape(NP, rows)], axis=1)
    pair = jnp.pad(pair, ((0, 0), (0, 14), (0, HD - rows)))
    body = (
        gate_up.astype(bf16).reshape(NP, rows, chunks, HD).transpose(0, 2, 1, 3)
    ).reshape(NP, chunks * rows, HD)
    summed = jnp.sum(swap(jnp.concatenate([body, pair], axis=1), "p").astype(f32), axis=0)
    square_sum = summed[chunks * rows] + summed[chunks * rows + 1]
    scale = lax.rsqrt(square_sum[:rows] / model + 1e-06)
    pre = summed[: chunks * rows].reshape(2, chunks // 2, rows, HD) * scale[:, None]
    activated = (jax.nn.silu(pre[0]) * pre[1]).astype(bf16)
    activated = share(activated, "p", NP).reshape(NP, chunks // 2, rows, HD)
    activated = activated.transpose(0, 2, 1, 3).reshape(total_slots, units)

    expert_out = jnp.concatenate(
        [dot(activated, block).astype(bf16) for block in weight_out], axis=1
    )
    returned = swap(expert_out.reshape(NPLANE, slots, width), PLANE).reshape(total_slots, width)
    combine_high = combine.astype(bf16)
    combine_low = (combine - combine_high.astype(f32)).astype(bf16)
    mixed = dot(combine_high, returned) + dot(combine_low, returned)
    mixed = mixed.astype(bf16)
    outgoing = jnp.stack(
        [
            lax.dynamic_slice_in_dim(mixed, jnp.bitwise_xor(q_index, k) * feat, feat, 1)
            for k in range(NQ)
        ]
    ).reshape(NQ * NZ, token_count, feat)
    landed = jnp.sum(swap(outgoing, ("q", "zh")).astype(f32), axis=0)
    stream = hidden[:, :feat].reshape(NCTX, NZ, share_rows, feat)
    stream = lax.dynamic_index_in_dim(stream, zh_index, 1, keepdims=False)
    return (stream.reshape(token_count, feat).astype(f32) + landed).astype(bf16)


def solution(mesh):
    fine = Mesh(mesh.devices.reshape(NP, NQ, NX, NZ, NY, NC), CTX + EXP)
    in_specs = (
        P(CTX, EXP),
        P(CTX, None),
        P(CTX + EXP, None),
        P(),
        P(EXP, None),
        P(EXP, None),
        P(EXP, None),
        P(EXP, CTX, None),
        P(EXP, None, CTX),
    )
    return jax.shard_map(
        shards, mesh=fine, in_specs=in_specs, out_specs=P(EXP, CTX), check_vma=False
    )
```

```python
import jax
import jax.numpy as jnp
from jax import lax
from jax.sharding import Mesh, PartitionSpec as P

HD = 128
KV_HEADS = 4
CAP = 5

NP, NQ = 4, 4
NX, NZ, NY, NC = 4, 2, 4, 2

CTX = ("p", "q")
EXP = ("x", "zh", "y", "core")
PLANE = ("x", "y", "core")
NPLANE = NX * NY * NC
NCTX = NP * NQ

masked_score = -1e30
f32 = jnp.float32
bf16 = jnp.bfloat16


def swap(array, axes):
    return lax.all_to_all(array, axes, split_axis=0, concat_axis=0, tiled=True)


def share(block, axes, count):
    return swap(jnp.broadcast_to(block[None], (count,) + block.shape), axes)


def dot(a, b):
    return jnp.dot(a, b, preferred_element_type=f32)


def from_neighbour(block, k):
    return lax.ppermute(block, "q", [(i, i ^ k) for i in range(NQ)])


def split(value):
    high = lax.reduce_precision(value, 8, 7)
    return high.astype(bf16), (value - high).astype(bf16)


def gather_column(keys_values, x_index):
    height = keys_values.shape[0] // (NY * NC)
    piece = lax.axis_index(("y", "core"))
    key_piece = lax.dynamic_slice(keys_values, (piece * height, x_index * HD), (height, HD))
    value_piece = lax.dynamic_slice(
        keys_values, (piece * height, (KV_HEADS + x_index) * HD), (height, HD)
    )
    return share(jnp.concatenate([key_piece, value_piece], axis=1), CTX, NCTX)


def key_positions(rows):
    height = rows // (NY * NC)
    number = jnp.arange(NCTX * rows, dtype=jnp.int32)
    return (
        (number % (NCTX * height)) // height * rows
        + number // (NCTX * height) * height
        + number % height
    )


def attend(queries, key_part, value_part, key_pos, ctx_index):
    rows = queries.shape[0]
    query_pos = ctx_index * rows + jnp.arange(rows, dtype=jnp.int32)
    scores = (
        jnp.einsum("qd,kd->qk", queries, key_part, preferred_element_type=f32) * HD ** (-0.5)
    )
    allowed = key_pos[None, :] <= query_pos[:, None]
    scores = jnp.where(allowed, scores, masked_score)
    top = jnp.max(scores, axis=-1, keepdims=True)
    weights = jnp.where(allowed, jnp.exp(scores - top), 0.0)
    total = jnp.sum(weights, axis=-1, keepdims=True)
    return (dot(weights.astype(bf16), value_part) / total).astype(bf16)


def shards(
    queries,
    keys_values,
    residual,
    norm_gain,
    out_weight,
    expert_ids,
    gate_values,
    gate_up_weight,
    down_weight,
):
    p_index = lax.axis_index("p")
    q_index = lax.axis_index("q")
    x_index = lax.axis_index("x")
    zh_index = lax.axis_index("zh")
    ctx_index = lax.axis_index(CTX)
    gate_up_weight = gate_up_weight[0]
    down_weight = down_weight[0]
    feat = down_weight.shape[1]
    units = down_weight.shape[0] // NQ
    width = NQ * feat
    model = NP * width

    def gate_up_block(target):
        gate = lax.dynamic_slice(gate_up_weight, (0, target * units), (feat, units))
        up = lax.dynamic_slice(gate_up_weight, (0, (NQ + target) * units), (feat, units))
        return jnp.concatenate([gate, up], axis=1)

    def down_block(target):
        return lax.dynamic_slice(down_weight, (target * units, 0), (units, feat))

    targets = [jnp.bitwise_xor(q_index, k) for k in range(NQ)]
    blocks_in = [gate_up_block(target) for target in targets]
    blocks_out = [down_block(target) for target in targets]
    weight_in = blocks_in[:1]
    weight_out = blocks_out[:1]
    early = tuple(range(1, NQ - 1))
    late = (NQ - 1,)

    def exchange(first, numbers):
        sent = [blocks_in[k] for k in numbers] + [blocks_out[k] for k in numbers]
        first, sent = lax.optimization_barrier((first, sent))
        moved = [from_neighbour(block, k) for block, k in zip(sent, numbers * 2)]
        return first, moved

    def keep(last, moved):
        last, moved = lax.optimization_barrier((last, moved))
        half = len(moved) // 2
        weight_in.extend(moved[:half])
        weight_out.extend(moved[half:])
        return last

    rows = keys_values.shape[0]
    column, moved = exchange(gather_column(keys_values, x_index), early)
    segment = keep(share(column, ("y", "core"), NY * NC), moved).reshape(NCTX * rows, 2 * HD)
    attended = attend(
        queries, segment[:, :HD], segment[:, HD:], key_positions(rows), ctx_index
    )
    attended, moved = exchange(attended, late)

    share_rows = attended.shape[0] // (NPLANE * NZ)
    attended = (
        attended.reshape(NX, NZ, NY, NC, share_rows, HD)
        .transpose(0, 2, 3, 1, 4, 5)
        .reshape(-1, HD)
    )
    partial = dot(attended, out_weight).astype(bf16).reshape(NPLANE, NZ * share_rows, model)
    partial = keep(swap(partial, PLANE), moved)
    partial = jnp.sum(partial.astype(f32), axis=0).reshape(NZ, share_rows, model)
    own_group = jnp.arange(NZ)[:, None, None] == zh_index
    partial = partial + jnp.where(own_group, residual.astype(f32)[None], 0.0)
    outgoing = partial.astype(bf16).reshape(NZ * share_rows, NP, width).transpose(1, 0, 2)

    routing = jnp.concatenate([expert_ids.astype(bf16), *split(gate_values)], axis=1)
    routing = lax.dynamic_slice_in_dim(routing, ctx_index * share_rows, share_rows, 0)
    routing = jnp.pad(routing, ((0, 0), (0, HD - routing.shape[1])))
    routing = jnp.where(own_group, routing[None], 0).reshape(1, NZ * share_rows, HD)
    routing = jnp.broadcast_to(routing, (NP,) + routing.shape[1:])
    outgoing = jnp.concatenate([outgoing, routing], axis=2)
    wide = width + HD
    outgoing = jnp.broadcast_to(
        outgoing[:, None, None], (NP, NQ, NZ, NZ * share_rows, wide)
    ).reshape(NCTX * NZ, NZ * share_rows, wide)
    arrived = swap(outgoing, CTX + ("zh",)).reshape(NCTX, NZ, NZ * share_rows, wide)
    arrived = jnp.sum(arrived.astype(f32), axis=1)
    hidden = arrived[:, :, :width].astype(bf16).reshape(-1, width)
    choices = expert_ids.shape[1]
    token_count = expert_ids.shape[0]
    routing = (
        arrived[:, :, width : width + 3 * choices]
        .reshape(NCTX, NZ, share_rows, 3, choices)
        .transpose(3, 1, 0, 2, 4)
        .reshape(3, NZ, token_count, choices)
    )

    hidden = jnp.concatenate(
        [
            lax.dynamic_slice_in_dim(hidden, jnp.bitwise_xor(q_index, k) * feat, feat, 1)
            for k in range(NQ)
        ],
        axis=1,
    )
    gain = jnp.concatenate(
        [
            lax.dynamic_slice_in_dim(
                norm_gain, (p_index * NQ + jnp.bitwise_xor(q_index, k)) * feat, feat, 0
            )
            for k in range(NQ)
        ]
    )

    ids = routing[0].astype(jnp.int32)
    number = jnp.arange(NPLANE, dtype=jnp.int32)
    experts = (number // (NY * NC) * NZ + zh_index) * (NY * NC) + number % (NY * NC)
    picked = ids[..., None] == experts
    chosen = jnp.sum(picked.astype(jnp.int32), axis=2)
    slot_index = jnp.cumsum(chosen, axis=1, dtype=jnp.int32) - chosen
    gate_tables = jnp.sum(jnp.where(picked, routing[1:, ..., None], 0.0), axis=3)
    placed = (chosen[..., None] > 0) & (
        slot_index[..., None] == jnp.arange(CAP, dtype=jnp.int32)
    )
    same = jnp.eye(NZ, dtype=bool)[:, :, None, None, None]
    spread = (placed[:, None] & same).astype(f32)
    slots = NZ * CAP
    total_slots = NPLANE * slots
    selector = (
        spread.astype(bf16)
        .reshape(NZ, NZ, NCTX, share_rows, NPLANE, CAP)
        .transpose(4, 1, 5, 2, 0, 3)
        .reshape(total_slots, NZ * token_count)
    )
    combine = (
        (spread * gate_tables[:, :, None, :, :, None])
        .transpose(0, 1, 3, 4, 2, 5)
        .reshape(2, NZ * token_count, total_slots)
        .astype(bf16)
    )

    buckets = dot(selector, hidden).astype(bf16).reshape(NPLANE, -1, HD)
    buffer = swap(buckets, PLANE).reshape(total_slots, width).astype(f32)
    squares = jnp.sum(buffer * buffer, axis=1)
    scaled = (buffer * gain).astype(bf16)
    gate_up = dot(scaled[:, :feat], weight_in[0])
    for k in range(1, NQ):
        gate_up = gate_up + dot(scaled[:, k * feat : (k + 1) * feat], weight_in[k])

    rows = total_slots // NP
    chunks = 2 * units // HD
    high, low = split(squares.reshape(NP, rows))
    pair = jnp.stack([high, low], axis=1)
    pair = jnp.pad(pair, ((0, 0), (0, 14), (0, HD - rows)))
    body = (
        gate_up.astype(bf16).reshape(NP, rows, chunks, HD).transpose(0, 2, 1, 3)
    ).reshape(NP, chunks * rows, HD)
    summed = jnp.sum(swap(jnp.concatenate([body, pair], axis=1), "p").astype(f32), axis=0)
    square_sum = summed[chunks * rows] + summed[chunks * rows + 1]
    scale = lax.rsqrt(square_sum[:rows] / model + 1e-06)
    pre = summed[: chunks * rows].reshape(2, chunks // 2, rows, HD) * scale[:, None]
    activated = (jax.nn.silu(pre[0]) * pre[1]).astype(bf16)
    activated = share(activated, "p", NP).reshape(NP, chunks // 2, rows, HD)
    activated = activated.transpose(0, 2, 1, 3).reshape(total_slots, units)

    expert_out = jnp.concatenate(
        [dot(activated, block).astype(bf16) for block in weight_out], axis=1
    )
    returned = swap(expert_out.reshape(NPLANE, -1, HD), PLANE).reshape(total_slots, width)
    mixed = dot(combine[0], returned) + dot(combine[1], returned)
    mixed = mixed.astype(bf16)
    outgoing = jnp.stack(
        [
            lax.dynamic_slice_in_dim(mixed, jnp.bitwise_xor(q_index, k) * feat, feat, 1)
            for k in range(NQ)
        ]
    ).reshape(NQ * NZ, token_count, feat)
    landed = jnp.sum(swap(outgoing, ("q", "zh")).astype(f32), axis=0)
    stream = hidden[:, :feat].reshape(NCTX, NZ, share_rows, feat)
    stream = lax.dynamic_index_in_dim(stream, zh_index, 1, keepdims=False)
    return (stream.reshape(token_count, feat).astype(f32) + landed).astype(bf16)


def solution(mesh):
    fine = Mesh(mesh.devices.reshape(NP, NQ, NX, NZ, NY, NC), CTX + EXP)
    in_specs = (
        P(CTX, EXP),
        P(CTX, None),
        P(CTX + EXP, None),
        P(),
        P(EXP, None),
        P(EXP, None),
        P(EXP, None),
        P(EXP, CTX, None),
        P(EXP, None, CTX),
    )
    return jax.shard_map(
        shards, mesh=fine, in_specs=in_specs, out_specs=P(EXP, CTX), check_vma=False
    )
```

```python
import jax
import jax.numpy as jnp
from jax import lax
from jax.sharding import Mesh, PartitionSpec as P

HD = 128
KV_HEADS = 4
CAP = 5

NP, NQ = 4, 4
NX, NZ, NY, NC = 4, 2, 4, 2

CTX = ("p", "q")
EXP = ("x", "zh", "y", "core")
PLANE = ("x", "y", "core")
NPLANE = NX * NY * NC
NCTX = NP * NQ

masked_score = -1e30
f32 = jnp.float32
bf16 = jnp.bfloat16


def swap(array, axes):
    return lax.all_to_all(array, axes, split_axis=0, concat_axis=0, tiled=True)


def share(block, axes, count):
    return swap(jnp.broadcast_to(block[None], (count,) + block.shape), axes)


def dot(a, b):
    return jnp.dot(a, b, preferred_element_type=f32)


def from_peer(block, axis, count, k):
    return lax.ppermute(block, axis, [(i, i ^ k) for i in range(count)])


def from_peers(blocks, axis, count):
    return [blocks[0]] + [from_peer(blocks[k], axis, count, k) for k in range(1, count)]


def add(blocks):
    total = blocks[0].astype(f32)
    for block in blocks[1:]:
        total = total + block.astype(f32)
    return total


def split(value):
    high = lax.reduce_precision(value, 8, 7)
    return high.astype(bf16), (value - high).astype(bf16)


def gather_column(keys_values, x_index):
    height = keys_values.shape[0] // (NY * NC)
    piece = lax.axis_index(("y", "core"))
    key_piece = lax.dynamic_slice(keys_values, (piece * height, x_index * HD), (height, HD))
    value_piece = lax.dynamic_slice(
        keys_values, (piece * height, (KV_HEADS + x_index) * HD), (height, HD)
    )
    return share(jnp.concatenate([key_piece, value_piece], axis=1), CTX, NCTX)


def key_positions(rows):
    height = rows // (NY * NC)
    core = jnp.bitwise_xor(jnp.arange(NC, dtype=jnp.int32), lax.axis_index("core"))
    y = jnp.bitwise_xor(jnp.arange(NY, dtype=jnp.int32), lax.axis_index("y"))
    piece = y[None, :] * NC + core[:, None]
    ctx = jnp.arange(NCTX, dtype=jnp.int32)[:, None]
    row = jnp.arange(height, dtype=jnp.int32)
    return (piece[:, :, None, None] * height + ctx * rows + row).reshape(-1)


def attend(queries, key_part, value_part, key_pos, ctx_index):
    rows = queries.shape[0]
    query_pos = ctx_index * rows + jnp.arange(rows, dtype=jnp.int32)
    scores = (
        jnp.einsum("qd,kd->qk", queries, key_part, preferred_element_type=f32) * HD ** (-0.5)
    )
    allowed = key_pos[None, :] <= query_pos[:, None]
    scores = jnp.where(allowed, scores, masked_score)
    top = jnp.max(scores, axis=-1, keepdims=True)
    weights = jnp.where(allowed, jnp.exp(scores - top), 0.0)
    total = jnp.sum(weights, axis=-1, keepdims=True)
    return (dot(weights.astype(bf16), value_part) / total).astype(bf16)


def shards(
    queries,
    keys_values,
    residual,
    norm_gain,
    out_weight,
    expert_ids,
    gate_values,
    gate_up_weight,
    down_weight,
):
    p_index = lax.axis_index("p")
    q_index = lax.axis_index("q")
    x_index = lax.axis_index("x")
    zh_index = lax.axis_index("zh")
    ctx_index = lax.axis_index(CTX)
    gate_up_weight = gate_up_weight[0]
    down_weight = down_weight[0]
    feat = down_weight.shape[1]
    units = down_weight.shape[0] // NQ
    width = NQ * feat
    model = NP * width

    def gate_up_block(target):
        gate = lax.dynamic_slice(gate_up_weight, (0, target * units), (feat, units))
        up = lax.dynamic_slice(gate_up_weight, (0, (NQ + target) * units), (feat, units))
        return jnp.concatenate([gate, up], axis=1)

    def down_block(target):
        return lax.dynamic_slice(down_weight, (target * units, 0), (units, feat))

    targets = [jnp.bitwise_xor(q_index, k) for k in range(NQ)]
    blocks_in = [gate_up_block(target) for target in targets]
    blocks_out = [down_block(target) for target in targets]
    moved_in = {0: blocks_in[0]}
    moved_out = {0: blocks_out[0]}

    def begin(first, into, out):
        sent = {"in": {k: blocks_in[k] for k in into}, "out": {k: blocks_out[k] for k in out}}
        first, sent = lax.optimization_barrier((first, sent))
        moved = jax.tree.map(lambda block: block, sent)
        for part in moved.values():
            for k in part:
                part[k] = from_peer(part[k], "q", NQ, k)
        return first, moved

    def end(last, moved):
        last, moved = lax.optimization_barrier((last, moved))
        moved_in.update(moved["in"])
        moved_out.update(moved["out"])
        return last

    half, rest = tuple(range(2, 2 + (NQ - 2) // 2)), tuple(range(2 + (NQ - 2) // 2, NQ))
    rows = keys_values.shape[0]
    keys_values, moved = begin(keys_values, (1,), (1,))
    column = end(gather_column(keys_values, x_index), moved)
    column, moved = begin(column, half, ())
    segment = jnp.concatenate(from_peers([column] * NY, "y", NY), axis=0)
    segment = jnp.concatenate(from_peers([segment] * NC, "core", NC), axis=0)
    segment = end(segment, moved).reshape(NCTX * rows, 2 * HD)
    attended = attend(
        queries, segment[:, :HD], segment[:, HD:], key_positions(rows), ctx_index
    )
    attended, moved = begin(attended, rest, ())

    share_rows = attended.shape[0] // (NPLANE * NZ)
    attended = (
        attended.reshape(NX, NZ, NY, NC, share_rows, HD)
        .transpose(0, 2, 3, 1, 4, 5)
        .reshape(-1, HD)
    )
    partial = dot(attended, out_weight).astype(bf16).reshape(NPLANE, NZ * share_rows, model)
    partial = end(swap(partial, PLANE), moved)
    partial = jnp.sum(partial.astype(f32), axis=0).reshape(NZ, share_rows, model)
    own_group = jnp.arange(NZ)[:, None, None] == zh_index
    partial = partial + jnp.where(own_group, residual.astype(f32)[None], 0.0)
    outgoing = partial.astype(bf16).reshape(NZ * share_rows, NCTX, feat).transpose(1, 0, 2)

    routing = jnp.concatenate([expert_ids.astype(bf16), *split(gate_values)], axis=1)
    routing = lax.dynamic_slice_in_dim(routing, ctx_index * share_rows, share_rows, 0)
    routing = jnp.pad(routing, ((0, 0), (0, HD - routing.shape[1])))
    routing = jnp.where(own_group, routing[None], 0).reshape(1, NZ * share_rows, HD)
    routing = jnp.broadcast_to(routing, (NCTX,) + routing.shape[1:])
    outgoing = jnp.concatenate([outgoing, routing], axis=2)
    wide = feat + HD
    outgoing = jnp.broadcast_to(
        outgoing[:, None], (NCTX, NZ, NZ * share_rows, wide)
    ).reshape(NCTX * NZ, NZ * share_rows, wide)
    arrived = swap(outgoing, CTX + ("zh",)).reshape(NCTX, NZ, NZ * share_rows, wide)
    arrived = jnp.sum(arrived.astype(f32), axis=1)
    hidden = arrived[:, :, :feat].astype(bf16).reshape(-1, feat)
    choices = expert_ids.shape[1]
    token_count = expert_ids.shape[0]
    routing = (
        arrived[:, :, feat : feat + 3 * choices]
        .reshape(NCTX, NZ, share_rows, 3, choices)
        .transpose(3, 1, 0, 2, 4)
        .reshape(3, NZ, token_count, choices)
    )

    hidden = jnp.concatenate(from_peers([hidden] * NQ, "q", NQ), axis=1)
    gain = jnp.concatenate(
        [
            lax.dynamic_slice_in_dim(
                norm_gain, (p_index * NQ + jnp.bitwise_xor(q_index, k)) * feat, feat, 0
            )
            for k in range(NQ)
        ]
    )

    ids = routing[0].astype(jnp.int32)
    number = jnp.arange(NPLANE, dtype=jnp.int32)
    experts = (number // (NY * NC) * NZ + zh_index) * (NY * NC) + number % (NY * NC)
    picked = ids[..., None] == experts
    chosen = jnp.sum(picked.astype(jnp.int32), axis=2)
    slot_index = jnp.cumsum(chosen, axis=1, dtype=jnp.int32) - chosen
    gate_tables = jnp.sum(jnp.where(picked, routing[1:, ..., None], 0.0), axis=3)
    placed = (chosen[..., None] > 0) & (
        slot_index[..., None] == jnp.arange(CAP, dtype=jnp.int32)
    )
    same = jnp.eye(NZ, dtype=bool)[:, :, None, None, None]
    spread = (placed[:, None] & same).astype(f32)
    slots = NZ * CAP
    total_slots = NPLANE * slots
    selector = (
        spread.astype(bf16)
        .reshape(NZ, NZ, NCTX, share_rows, NPLANE, CAP)
        .transpose(4, 1, 5, 2, 0, 3)
        .reshape(total_slots, NZ * token_count)
    )
    combine = (
        (spread * gate_tables[:, :, None, :, :, None])
        .transpose(0, 1, 3, 4, 2, 5)
        .reshape(2, NZ * token_count, total_slots)
        .astype(bf16)
    )

    buckets = dot(selector, hidden).astype(bf16).reshape(NPLANE, -1, HD)
    buckets, moved = begin(buckets, (), half + rest)
    buffer = end(swap(buckets, PLANE), moved).reshape(total_slots, width).astype(f32)
    squares = jnp.sum(buffer * buffer, axis=1)
    scaled = (buffer * gain).astype(bf16)
    gate_up = dot(scaled[:, :feat], moved_in[0])
    for k in range(1, NQ):
        gate_up = gate_up + dot(scaled[:, k * feat : (k + 1) * feat], moved_in[k])

    rows = total_slots // NP
    chunks = 2 * units // HD
    high, low = split(squares.reshape(NP, rows))
    pair = jnp.stack([high, low], axis=1)
    pair = jnp.pad(pair, ((0, 0), (0, 14), (0, HD - rows)))
    body = (
        gate_up.astype(bf16).reshape(NP, rows, chunks, HD).transpose(0, 2, 1, 3)
    ).reshape(NP, chunks * rows, HD)
    body = jnp.concatenate([body, pair], axis=1)
    parts = [
        lax.dynamic_index_in_dim(body, jnp.bitwise_xor(p_index, k), 0, keepdims=False)
        for k in range(NP)
    ]
    summed = add(from_peers(parts, "p", NP))
    square_sum = summed[chunks * rows] + summed[chunks * rows + 1]
    scale = lax.rsqrt(square_sum[:rows] / model + 1e-06)
    pre = summed[: chunks * rows].reshape(2, chunks // 2, rows, HD) * scale[:, None]
    activated = (jax.nn.silu(pre[0]) * pre[1]).astype(bf16)
    activated = jnp.stack(from_peers([activated] * NP, "p", NP))
    activated = jnp.stack(
        [
            lax.dynamic_index_in_dim(activated, jnp.bitwise_xor(p_index, k), 0, keepdims=False)
            for k in range(NP)
        ]
    )
    activated = activated.transpose(0, 2, 1, 3).reshape(total_slots, units)

    expert_out = jnp.concatenate(
        [dot(activated, moved_out[k]).astype(bf16) for k in range(NQ)], axis=1
    )
    returned = swap(expert_out.reshape(NPLANE, -1, HD), PLANE).reshape(total_slots, width)
    mixed = dot(combine[0], returned) + dot(combine[1], returned)
    parts = [mixed[:, k * feat : (k + 1) * feat] for k in range(NQ)]
    landed = add(from_peers(parts[:1] + [part.astype(bf16) for part in parts[1:]], "q", NQ))
    landed = landed.reshape(NZ, token_count, feat)
    passed = lax.dynamic_index_in_dim(landed, NZ - 1 - zh_index, 0, keepdims=False)
    passed = from_peer(passed.astype(bf16), "zh", NZ, 1)
    landed = lax.dynamic_index_in_dim(landed, zh_index, 0, keepdims=False) + passed.astype(f32)
    stream = hidden[:, :feat].reshape(NCTX, NZ, share_rows, feat)
    stream = lax.dynamic_index_in_dim(stream, zh_index, 1, keepdims=False)
    return (stream.reshape(token_count, feat).astype(f32) + landed).astype(bf16)


def solution(mesh):
    fine = Mesh(mesh.devices.reshape(NP, NQ, NX, NZ, NY, NC), CTX + EXP)
    in_specs = (
        P(CTX, EXP),
        P(CTX, None),
        P(CTX + EXP, None),
        P(),
        P(EXP, None),
        P(EXP, None),
        P(EXP, None),
        P(EXP, CTX, None),
        P(EXP, None, CTX),
    )
    return jax.shard_map(
        shards, mesh=fine, in_specs=in_specs, out_specs=P(EXP, CTX), check_vma=False
    )
```

```python
import jax
import jax.numpy as jnp
from jax import lax
from jax.experimental import pallas as pl
from jax.experimental.pallas import tpu as pltpu
from jax.sharding import Mesh, PartitionSpec as P

HD = 128
KV_HEADS = 4
CAP = 5

NP, NQ = 4, 4
NX, NZ, NY, NC = 4, 2, 4, 2

CTX = ("p", "q")
EXP = ("x", "zh", "y", "core")
PLANE = ("x", "y", "core")
NPLANE = NX * NY * NC
NCTX = NP * NQ

masked_score = -1e30
f32 = jnp.float32
bf16 = jnp.bfloat16


def swap(array, axes):
    return lax.all_to_all(array, axes, split_axis=0, concat_axis=0, tiled=True)


def share(block, axes, count):
    return swap(jnp.broadcast_to(block[None], (count,) + block.shape), axes)


def dot(a, b):
    return jnp.dot(a, b, preferred_element_type=f32)


def from_peer(block, axis, count, k):
    return lax.ppermute(block, axis, [(i, i ^ k) for i in range(count)])


def from_peers(blocks, axis, count):
    return [blocks[0]] + [from_peer(blocks[k], axis, count, k) for k in range(1, count)]


def add(blocks):
    total = blocks[0].astype(f32)
    for block in blocks[1:]:
        total = total + block.astype(f32)
    return total


def split(value):
    high = lax.reduce_precision(value, 8, 7)
    return high.astype(bf16), (value - high).astype(bf16)


def gather_column(keys_values, x_index):
    height = keys_values.shape[0] // (NY * NC)
    piece = lax.axis_index(("y", "core"))
    key_piece = lax.dynamic_slice(keys_values, (piece * height, x_index * HD), (height, HD))
    value_piece = lax.dynamic_slice(
        keys_values, (piece * height, (KV_HEADS + x_index) * HD), (height, HD)
    )
    return share(jnp.concatenate([key_piece, value_piece], axis=1), CTX, NCTX)


def key_positions(rows):
    height = rows // (NY * NC)
    number = jnp.arange(NCTX * rows, dtype=jnp.int32)
    return (
        (number % (NCTX * height)) // height * rows
        + number // (NCTX * height) * height
        + number % height
    )


def call(kernel, shape, *operands):
    return pl.pallas_call(
        kernel,
        out_shape=jax.ShapeDtypeStruct(shape, bf16),
        compiler_params=pltpu.CompilerParams(vmem_limit_bytes=32 * 1024 * 1024),
    )(*operands)


def gate_up_kernel(buffer_ref, gain_ref, *refs):
    out_ref = refs[-1]
    feat, units = refs[0].shape
    rows = buffer_ref.shape[0] // NP
    buffer = buffer_ref[...].astype(f32)
    squares = jnp.sum(buffer * buffer, axis=1, keepdims=True)
    scaled = (buffer * gain_ref[...]).astype(bf16)
    for half in range(2):
        total = dot(scaled[:, :feat], refs[half * NQ][...])
        for k in range(1, NQ):
            total = total + dot(scaled[:, k * feat : (k + 1) * feat], refs[half * NQ + k][...])
        total = total.astype(bf16)
        for p in range(NP):
            for chunk in range(units // HD):
                start = (half * (units // HD) + chunk) * rows
                out_ref[p, start : start + rows, :] = total[
                    p * rows : (p + 1) * rows, chunk * HD : (chunk + 1) * HD
                ]
    body = 2 * (units // HD) * rows
    lane = lax.broadcasted_iota(jnp.int32, (rows, HD), 1)
    on_diagonal = lane == lax.broadcasted_iota(jnp.int32, (rows, HD), 0)
    row = lax.broadcasted_iota(jnp.int32, (16, HD), 0)
    for p in range(NP):
        column = jnp.broadcast_to(squares[p * rows : (p + 1) * rows], (rows, HD))
        line = jnp.sum(jnp.where(on_diagonal, column, 0.0), axis=0, keepdims=True)
        high = line.astype(bf16).astype(f32)
        pair = jnp.where(row == 0, high, jnp.where(row == 1, line - high, 0.0))
        out_ref[p, body : body + 16, :] = pair.astype(bf16)


def down_kernel(activated_ref, *refs):
    out_ref = refs[-1]
    parts, chunks, rows, _ = activated_ref.shape
    feat = refs[0].shape[1]
    activated = jnp.concatenate(
        [
            jnp.concatenate([activated_ref[p, chunk] for chunk in range(chunks)], axis=1)
            for p in range(parts)
        ],
        axis=0,
    )
    for k in range(NQ):
        out_ref[:, k * feat : (k + 1) * feat] = dot(activated, refs[k][...]).astype(bf16)


def attend(queries, key_part, value_part, key_pos, ctx_index):
    rows = queries.shape[0]
    query_pos = ctx_index * rows + jnp.arange(rows, dtype=jnp.int32)
    scores = (
        jnp.einsum("qd,kd->qk", queries, key_part, preferred_element_type=f32) * HD ** (-0.5)
    )
    allowed = key_pos[None, :] <= query_pos[:, None]
    scores = jnp.where(allowed, scores, masked_score)
    top = jnp.max(scores, axis=-1, keepdims=True)
    weights = jnp.where(allowed, jnp.exp(scores - top), 0.0)
    total = jnp.sum(weights, axis=-1, keepdims=True)
    return (dot(weights.astype(bf16), value_part) / total).astype(bf16)


def shards(
    queries,
    keys_values,
    residual,
    norm_gain,
    out_weight,
    expert_ids,
    gate_values,
    gate_up_weight,
    down_weight,
):
    p_index = lax.axis_index("p")
    q_index = lax.axis_index("q")
    x_index = lax.axis_index("x")
    zh_index = lax.axis_index("zh")
    ctx_index = lax.axis_index(CTX)
    gate_up_weight = gate_up_weight[0]
    down_weight = down_weight[0]
    feat = down_weight.shape[1]
    units = down_weight.shape[0] // NQ
    width = NQ * feat
    model = NP * width

    def gate_block(target):
        return lax.dynamic_slice(gate_up_weight, (0, target * units), (feat, units))

    def up_block(target):
        return lax.dynamic_slice(gate_up_weight, (0, (NQ + target) * units), (feat, units))

    def down_block(target):
        return lax.dynamic_slice(down_weight, (target * units, 0), (units, feat))

    targets = [jnp.bitwise_xor(q_index, k) for k in range(NQ)]
    sent = {
        name: [block(target) for target in targets]
        for name, block in (("gate", gate_block), ("up", up_block), ("down", down_block))
    }
    moved = {(name, 0): blocks[0] for name, blocks in sent.items()}

    def begin(first, *units_sent):
        blocks = [sent[name][k] for name, k in units_sent]
        first, blocks = lax.optimization_barrier((first, blocks))
        arriving = [from_peer(block, "q", NQ, k) for block, (_, k) in zip(blocks, units_sent)]
        return first, (units_sent, arriving)

    def end(last, flight):
        units_sent, arriving = flight
        last, arriving = lax.optimization_barrier((last, arriving))
        moved.update(zip(units_sent, arriving))
        return last

    rows = keys_values.shape[0]
    keys_values, flight = begin(
        keys_values, ("gate", 1), ("up", 1), ("down", 1), ("gate", 2)
    )
    column = end(gather_column(keys_values, x_index), flight)
    column, flight = begin(column, ("up", 2))
    segment = end(share(column, ("y", "core"), NY * NC), flight).reshape(NCTX * rows, 2 * HD)
    attended = attend(
        queries, segment[:, :HD], segment[:, HD:], key_positions(rows), ctx_index
    )
    attended, flight = begin(attended, ("gate", 3), ("up", 3))

    share_rows = attended.shape[0] // (NPLANE * NZ)
    attended = (
        attended.reshape(NX, NZ, NY, NC, share_rows, HD)
        .transpose(0, 2, 3, 1, 4, 5)
        .reshape(-1, HD)
    )
    partial = dot(attended, out_weight).astype(bf16).reshape(NPLANE, NZ * share_rows, model)
    partial = end(swap(partial, PLANE), flight)
    partial = jnp.sum(partial.astype(f32), axis=0).reshape(NZ, share_rows, model)
    own_group = jnp.arange(NZ)[:, None, None] == zh_index
    partial = partial + jnp.where(own_group, residual.astype(f32)[None], 0.0)
    outgoing = partial.astype(bf16).reshape(NZ * share_rows, NCTX, feat).transpose(1, 0, 2)

    routing = jnp.concatenate([expert_ids.astype(bf16), *split(gate_values)], axis=1)
    routing = lax.dynamic_slice_in_dim(routing, ctx_index * share_rows, share_rows, 0)
    routing = jnp.pad(routing, ((0, 0), (0, HD - routing.shape[1])))
    routing = jnp.where(own_group, routing[None], 0).reshape(1, NZ * share_rows, HD)
    routing = jnp.broadcast_to(routing, (NCTX,) + routing.shape[1:])
    outgoing = jnp.concatenate([outgoing, routing], axis=2)
    outgoing, flight = begin(outgoing, ("down", 2))
    wide = feat + HD
    outgoing = jnp.broadcast_to(
        outgoing[:, None], (NCTX, NZ, NZ * share_rows, wide)
    ).reshape(NCTX * NZ, NZ * share_rows, wide)
    arrived = swap(outgoing, CTX + ("zh",)).reshape(NCTX, NZ, NZ * share_rows, wide)
    arrived = jnp.sum(arrived.astype(f32), axis=1)
    hidden = arrived[:, :, :feat].astype(bf16).reshape(-1, feat)
    choices = expert_ids.shape[1]
    token_count = expert_ids.shape[0]
    routing = (
        arrived[:, :, feat : feat + 3 * choices]
        .reshape(NCTX, NZ, share_rows, 3, choices)
        .transpose(3, 1, 0, 2, 4)
        .reshape(3, NZ, token_count, choices)
    )

    hidden = end(jnp.concatenate(from_peers([hidden] * NQ, "q", NQ), axis=1), flight)
    gain = jnp.concatenate(
        [
            lax.dynamic_slice_in_dim(
                norm_gain, (p_index * NQ + jnp.bitwise_xor(q_index, k)) * feat, feat, 0
            )
            for k in range(NQ)
        ]
    )

    ids = routing[0].astype(jnp.int32)
    number = jnp.arange(NPLANE, dtype=jnp.int32)
    experts = (number // (NY * NC) * NZ + zh_index) * (NY * NC) + number % (NY * NC)
    picked = ids[..., None] == experts
    chosen = jnp.sum(picked.astype(jnp.int32), axis=2)
    slot_index = jnp.cumsum(chosen, axis=1, dtype=jnp.int32) - chosen
    gate_tables = jnp.sum(jnp.where(picked, routing[1:, ..., None], 0.0), axis=3)
    placed = (chosen[..., None] > 0) & (
        slot_index[..., None] == jnp.arange(CAP, dtype=jnp.int32)
    )
    same = jnp.eye(NZ, dtype=bool)[:, :, None, None, None]
    spread = (placed[:, None] & same).astype(f32)
    slots = NZ * CAP
    total_slots = NPLANE * slots
    selector = (
        spread.astype(bf16)
        .reshape(NZ, NZ, NCTX, share_rows, NPLANE, CAP)
        .transpose(4, 1, 5, 2, 0, 3)
        .reshape(total_slots, NZ * token_count)
    )
    combine = (
        (spread * gate_tables[:, :, None, :, :, None])
        .transpose(0, 1, 3, 4, 2, 5)
        .reshape(2, NZ * token_count, total_slots)
        .astype(bf16)
    )

    buckets = dot(selector, hidden).astype(bf16).reshape(NPLANE, -1, HD)
    buckets, flight = begin(buckets, ("down", 3))
    buffer = end(swap(buckets, PLANE), flight).reshape(total_slots, width)

    rows = total_slots // NP
    chunks = 2 * units // HD
    names = [(name, k) for name in ("gate", "up") for k in range(NQ)]
    body = call(
        gate_up_kernel,
        (NP, chunks * rows + 16, HD),
        buffer,
        gain[None],
        *[moved[name] for name in names],
    )
    parts = [
        lax.dynamic_index_in_dim(body, jnp.bitwise_xor(p_index, k), 0, keepdims=False)
        for k in range(NP)
    ]
    summed = add(from_peers(parts, "p", NP))
    square_sum = summed[chunks * rows] + summed[chunks * rows + 1]
    scale = lax.rsqrt(square_sum[:rows] / model + 1e-06)
    pre = summed[: chunks * rows].reshape(2, chunks // 2, rows, HD) * scale[:, None]
    activated = (jax.nn.silu(pre[0]) * pre[1]).astype(bf16)
    activated = share(activated, "p", NP)
    expert_out = call(
        down_kernel,
        (total_slots, width),
        activated.reshape(NP, chunks // 2, rows, HD),
        *[moved["down", k] for k in range(NQ)],
    )
    returned = swap(expert_out.reshape(NPLANE, -1, HD), PLANE).reshape(total_slots, width)
    mixed = dot(combine[0], returned) + dot(combine[1], returned)
    parts = [mixed[:, k * feat : (k + 1) * feat] for k in range(NQ)]
    landed = add(from_peers(parts[:1] + [part.astype(bf16) for part in parts[1:]], "q", NQ))
    landed = landed.reshape(NZ, token_count, feat)
    passed = lax.dynamic_index_in_dim(landed, NZ - 1 - zh_index, 0, keepdims=False)
    passed = from_peer(passed.astype(bf16), "zh", NZ, 1)
    landed = lax.dynamic_index_in_dim(landed, zh_index, 0, keepdims=False) + passed.astype(f32)
    stream = hidden[:, :feat].reshape(NCTX, NZ, share_rows, feat)
    stream = lax.dynamic_index_in_dim(stream, zh_index, 1, keepdims=False)
    return (stream.reshape(token_count, feat).astype(f32) + landed).astype(bf16)


def solution(mesh):
    fine = Mesh(mesh.devices.reshape(NP, NQ, NX, NZ, NY, NC), CTX + EXP)
    in_specs = (
        P(CTX, EXP),
        P(CTX, None),
        P(CTX + EXP, None),
        P(),
        P(EXP, None),
        P(EXP, None),
        P(EXP, None),
        P(EXP, CTX, None),
        P(EXP, None, CTX),
    )
    return jax.shard_map(
        shards, mesh=fine, in_specs=in_specs, out_specs=P(EXP, CTX), check_vma=False
    )
```

```python
import jax
import jax.numpy as jnp
from jax import lax
from jax.experimental import pallas as pl
from jax.experimental.pallas import tpu as pltpu
from jax.sharding import Mesh, PartitionSpec as P

HD = 128
KV_HEADS = 4
CAP = 5

NP, NQ = 4, 4
NX, NZ, NY, NC = 4, 2, 4, 2

CTX = ("p", "q")
EXP = ("x", "zh", "y", "core")
PLANE = ("x", "y", "core")
NPLANE = NX * NY * NC
NCTX = NP * NQ

masked_score = -1e30
f32 = jnp.float32
bf16 = jnp.bfloat16


def swap(array, axes):
    return lax.all_to_all(array, axes, split_axis=0, concat_axis=0, tiled=True)


def share(block, axes, count):
    return swap(jnp.broadcast_to(block[None], (count,) + block.shape), axes)


def dot(a, b):
    return jnp.dot(a, b, preferred_element_type=f32)


def from_peer(block, axis, count, k):
    return lax.ppermute(block, axis, [(i, i ^ k) for i in range(count)])


def from_peers(blocks, axis, count):
    return [blocks[0]] + [from_peer(blocks[k], axis, count, k) for k in range(1, count)]


def add(blocks):
    total = blocks[0].astype(f32)
    for block in blocks[1:]:
        total = total + block.astype(f32)
    return total


def split(value):
    high = lax.reduce_precision(value, 8, 7)
    return high.astype(bf16), (value - high).astype(bf16)


def gather_column(keys_values, x_index):
    height = keys_values.shape[0] // (NY * NC)
    piece = lax.axis_index(("y", "core"))
    key_piece = lax.dynamic_slice(keys_values, (piece * height, x_index * HD), (height, HD))
    value_piece = lax.dynamic_slice(
        keys_values, (piece * height, (KV_HEADS + x_index) * HD), (height, HD)
    )
    return share(jnp.concatenate([key_piece, value_piece], axis=1), CTX, NCTX)


def key_positions(rows):
    height = rows // (NY * NC)
    number = jnp.arange(NCTX * rows, dtype=jnp.int32)
    return (
        (number % (NCTX * height)) // height * rows
        + number // (NCTX * height) * height
        + number % height
    )


def call(kernel, shape, operands, weights):
    return pl.pallas_call(
        kernel,
        out_shape=jax.ShapeDtypeStruct(shape, bf16),
        in_specs=[pl.BlockSpec(memory_space=pltpu.VMEM)] * len(operands)
        + [pl.BlockSpec(memory_space=pl.ANY)] * len(weights),
        out_specs=pl.BlockSpec(memory_space=pltpu.VMEM),
        scratch_shapes=[
            pltpu.VMEM((len(weights),) + weights[0].shape, bf16),
            pltpu.SemaphoreType.DMA((len(weights),)),
        ],
        compiler_params=pltpu.CompilerParams(vmem_limit_bytes=32 * 1024 * 1024),
    )(*operands, *weights)


def fetch(weights, held, semaphores):
    copies = [
        pltpu.make_async_copy(weight, held.at[i], semaphores.at[i])
        for i, weight in enumerate(weights)
    ]
    for copy in copies:
        copy.start()
    return copies


def gate_up_kernel(buffer_ref, gain_ref, *refs):
    *weights, out_ref, held, semaphores = refs
    copies = fetch(weights, held, semaphores)
    _, feat, units = held.shape
    rows = buffer_ref.shape[0] // NP
    buffer = buffer_ref[...].astype(f32)
    squares = jnp.sum(buffer * buffer, axis=1, keepdims=True)
    scaled = (buffer * gain_ref[...]).astype(bf16)
    for half in range(2):
        total = jnp.zeros((buffer.shape[0], units), f32)
        for k in range(NQ):
            copies[half * NQ + k].wait()
            total = total + dot(scaled[:, k * feat : (k + 1) * feat], held[half * NQ + k])
        total = total.astype(bf16)
        for p in range(NP):
            for chunk in range(units // HD):
                start = (half * (units // HD) + chunk) * rows
                out_ref[p, start : start + rows, :] = total[
                    p * rows : (p + 1) * rows, chunk * HD : (chunk + 1) * HD
                ]
    body = 2 * (units // HD) * rows
    lane = lax.broadcasted_iota(jnp.int32, (rows, HD), 1)
    on_diagonal = lane == lax.broadcasted_iota(jnp.int32, (rows, HD), 0)
    row = lax.broadcasted_iota(jnp.int32, (16, HD), 0)
    for p in range(NP):
        column = jnp.broadcast_to(squares[p * rows : (p + 1) * rows], (rows, HD))
        line = jnp.sum(jnp.where(on_diagonal, column, 0.0), axis=0, keepdims=True)
        high = line.astype(bf16).astype(f32)
        pair = jnp.where(row == 0, high, jnp.where(row == 1, line - high, 0.0))
        out_ref[p, body : body + 16, :] = pair.astype(bf16)


def down_kernel(activated_ref, *refs):
    *weights, out_ref, held, semaphores = refs
    copies = fetch(weights, held, semaphores)
    parts, chunks, rows, _ = activated_ref.shape
    feat = held.shape[2]
    activated = jnp.concatenate(
        [
            jnp.concatenate([activated_ref[p, chunk] for chunk in range(chunks)], axis=1)
            for p in range(parts)
        ],
        axis=0,
    )
    for k in range(NQ):
        copies[k].wait()
        out_ref[:, k * feat : (k + 1) * feat] = dot(activated, held[k]).astype(bf16)


def attend(queries, key_part, value_part, key_pos, ctx_index):
    rows = queries.shape[0]
    query_pos = ctx_index * rows + jnp.arange(rows, dtype=jnp.int32)
    scores = (
        jnp.einsum("qd,kd->qk", queries, key_part, preferred_element_type=f32) * HD ** (-0.5)
    )
    allowed = key_pos[None, :] <= query_pos[:, None]
    scores = jnp.where(allowed, scores, masked_score)
    top = jnp.max(scores, axis=-1, keepdims=True)
    weights = jnp.where(allowed, jnp.exp(scores - top), 0.0)
    total = jnp.sum(weights, axis=-1, keepdims=True)
    return (dot(weights.astype(bf16), value_part) / total).astype(bf16)


def shards(
    queries,
    keys_values,
    residual,
    norm_gain,
    out_weight,
    expert_ids,
    gate_values,
    gate_up_weight,
    down_weight,
):
    p_index = lax.axis_index("p")
    q_index = lax.axis_index("q")
    x_index = lax.axis_index("x")
    zh_index = lax.axis_index("zh")
    ctx_index = lax.axis_index(CTX)
    gate_up_weight = gate_up_weight[0]
    down_weight = down_weight[0]
    feat = down_weight.shape[1]
    units = down_weight.shape[0] // NQ
    width = NQ * feat
    model = NP * width

    def gate_block(target):
        return lax.dynamic_slice(gate_up_weight, (0, target * units), (feat, units))

    def up_block(target):
        return lax.dynamic_slice(gate_up_weight, (0, (NQ + target) * units), (feat, units))

    def down_block(target):
        return lax.dynamic_slice(down_weight, (target * units, 0), (units, feat))

    targets = [jnp.bitwise_xor(q_index, k) for k in range(NQ)]
    sent = {
        name: [block(target) for target in targets]
        for name, block in (("gate", gate_block), ("up", up_block), ("down", down_block))
    }
    moved = {(name, 0): blocks[0] for name, blocks in sent.items()}

    def begin(first, *units_sent):
        blocks = [sent[name][k] for name, k in units_sent]
        if first is not None:
            first, blocks = lax.optimization_barrier((first, blocks))
        arriving = [from_peer(block, "q", NQ, k) for block, (_, k) in zip(blocks, units_sent)]
        return first, (units_sent, arriving)

    def end(last, flight):
        units_sent, arriving = flight
        last, arriving = lax.optimization_barrier((last, arriving))
        moved.update(zip(units_sent, arriving))
        return last

    rows = keys_values.shape[0]
    _, flight = begin(None, ("gate", 1), ("up", 1), ("gate", 2))
    column = end(gather_column(keys_values, x_index), flight)
    column, flight = begin(column, ("up", 2))
    segment = end(share(column, ("y", "core"), NY * NC), flight).reshape(NCTX * rows, 2 * HD)
    attended = attend(
        queries, segment[:, :HD], segment[:, HD:], key_positions(rows), ctx_index
    )
    attended, flight = begin(attended, ("gate", 3), ("up", 3))

    share_rows = attended.shape[0] // (NPLANE * NZ)
    attended = (
        attended.reshape(NX, NZ, NY, NC, share_rows, HD)
        .transpose(0, 2, 3, 1, 4, 5)
        .reshape(-1, HD)
    )
    partial = dot(attended, out_weight).astype(bf16).reshape(NPLANE, NZ * share_rows, model)
    partial = end(swap(partial, PLANE), flight)
    partial = jnp.sum(partial.astype(f32), axis=0).reshape(NZ, share_rows, model)
    own_group = jnp.arange(NZ)[:, None, None] == zh_index
    partial = partial + jnp.where(own_group, residual.astype(f32)[None], 0.0)
    outgoing = partial.astype(bf16).reshape(NZ * share_rows, NCTX, feat).transpose(1, 0, 2)

    routing = jnp.concatenate([expert_ids.astype(bf16), *split(gate_values)], axis=1)
    outgoing, routing = lax.optimization_barrier((outgoing, routing))
    other = from_peer(routing, "zh", NZ, 1)
    first = zh_index == 0
    routing = jnp.stack([jnp.where(first, routing, other), jnp.where(first, other, routing)])
    outgoing, flight = begin(outgoing, ("down", 1), ("down", 2), ("down", 3))
    outgoing = jnp.broadcast_to(
        outgoing[:, None], (NCTX, NZ, NZ * share_rows, feat)
    ).reshape(NCTX * NZ, NZ * share_rows, feat)
    arrived = swap(outgoing, CTX + ("zh",)).reshape(NCTX, NZ, NZ * share_rows, feat)
    arrived = end(arrived, flight).astype(f32)
    hidden = jnp.sum(arrived, axis=1).astype(bf16).reshape(-1, feat)
    choices = expert_ids.shape[1]
    token_count = expert_ids.shape[0]
    routing = routing.reshape(NZ, token_count, 3, choices).transpose(2, 0, 1, 3).astype(f32)

    hidden = jnp.concatenate(from_peers([hidden] * NQ, "q", NQ), axis=1)
    gain = jnp.concatenate(
        [
            lax.dynamic_slice_in_dim(
                norm_gain, (p_index * NQ + jnp.bitwise_xor(q_index, k)) * feat, feat, 0
            )
            for k in range(NQ)
        ]
    )

    ids = routing[0].astype(jnp.int32)
    number = jnp.arange(NPLANE, dtype=jnp.int32)
    experts = (number // (NY * NC) * NZ + zh_index) * (NY * NC) + number % (NY * NC)
    picked = ids[..., None] == experts
    chosen = jnp.sum(picked.astype(jnp.int32), axis=2)
    slot_index = jnp.cumsum(chosen, axis=1, dtype=jnp.int32) - chosen
    gate_tables = jnp.sum(jnp.where(picked, routing[1:, ..., None], 0.0), axis=3)
    placed = (chosen[..., None] > 0) & (
        slot_index[..., None] == jnp.arange(CAP, dtype=jnp.int32)
    )
    same = jnp.eye(NZ, dtype=bool)[:, :, None, None, None]
    spread = (placed[:, None] & same).astype(f32)
    slots = NZ * CAP
    total_slots = NPLANE * slots
    selector = (
        spread.astype(bf16)
        .reshape(NZ, NZ, NCTX, share_rows, NPLANE, CAP)
        .transpose(4, 1, 5, 2, 0, 3)
        .reshape(total_slots, NZ * token_count)
    )
    combine = (
        (spread * gate_tables[:, :, None, :, :, None])
        .transpose(0, 1, 3, 4, 2, 5)
        .reshape(2, NZ * token_count, total_slots)
        .astype(bf16)
    )

    buckets = dot(selector, hidden).astype(bf16).reshape(NPLANE, -1, HD)
    buffer = swap(buckets, PLANE).reshape(total_slots, width)

    rows = total_slots // NP
    chunks = 2 * units // HD
    names = [(name, k) for name in ("gate", "up") for k in range(NQ)]
    body = call(
        gate_up_kernel,
        (NP, chunks * rows + 16, HD),
        (buffer, gain[None]),
        [moved[name] for name in names],
    )
    parts = [
        lax.dynamic_index_in_dim(body, jnp.bitwise_xor(p_index, k), 0, keepdims=False)
        for k in range(NP)
    ]
    summed = add(from_peers(parts, "p", NP))
    square_sum = summed[chunks * rows] + summed[chunks * rows + 1]
    scale = lax.rsqrt(square_sum[:rows] / model + 1e-06)
    pre = summed[: chunks * rows].reshape(2, chunks // 2, rows, HD) * scale[:, None]
    activated = (jax.nn.silu(pre[0]) * pre[1]).astype(bf16)
    activated = share(activated, "p", NP)
    expert_out = call(
        down_kernel,
        (total_slots, width),
        (activated.reshape(NP, chunks // 2, rows, HD),),
        [moved["down", k] for k in range(NQ)],
    )
    returned = swap(expert_out.reshape(NPLANE, -1, HD), PLANE).reshape(total_slots, width)
    mixed = dot(combine[0], returned) + dot(combine[1], returned)
    parts = [mixed[:, k * feat : (k + 1) * feat] for k in range(NQ)]
    landed = add(from_peers(parts[:1] + [part.astype(bf16) for part in parts[1:]], "q", NQ))
    landed = landed.reshape(NZ, token_count, feat)
    passed = lax.dynamic_index_in_dim(landed, NZ - 1 - zh_index, 0, keepdims=False)
    passed = from_peer(passed.astype(bf16), "zh", NZ, 1)
    landed = lax.dynamic_index_in_dim(landed, zh_index, 0, keepdims=False) + passed.astype(f32)
    stream = hidden[:, :feat].reshape(NCTX, NZ, share_rows, feat)
    stream = lax.dynamic_index_in_dim(stream, zh_index, 1, keepdims=False)
    return (stream.reshape(token_count, feat).astype(f32) + landed).astype(bf16)


def solution(mesh):
    fine = Mesh(mesh.devices.reshape(NP, NQ, NX, NZ, NY, NC), CTX + EXP)
    in_specs = (
        P(CTX, EXP),
        P(CTX, None),
        P(CTX + EXP, None),
        P(),
        P(EXP, None),
        P(EXP, None),
        P(EXP, None),
        P(EXP, CTX, None),
        P(EXP, None, CTX),
    )
    return jax.shard_map(
        shards, mesh=fine, in_specs=in_specs, out_specs=P(EXP, CTX), check_vma=False
    )
```

```python
import jax
import jax.numpy as jnp
from jax import lax
from jax.experimental import pallas as pl
from jax.experimental.pallas import tpu as pltpu
from jax.sharding import Mesh, PartitionSpec as P

HD = 128
KV_HEADS = 4
CAP = 5

NP, NQ = 4, 4
NX, NZ, NY, NC = 4, 2, 4, 2

CTX = ("p", "q")
EXP = ("x", "zh", "y", "core")
PLANE = ("x", "y", "core")
NPLANE = NX * NY * NC
NCTX = NP * NQ

masked_score = -1e30
f32 = jnp.float32
bf16 = jnp.bfloat16


def swap(array, axes):
    return lax.all_to_all(array, axes, split_axis=0, concat_axis=0, tiled=True)


def share(block, axes, count):
    return swap(jnp.broadcast_to(block[None], (count,) + block.shape), axes)


def dot(a, b):
    return jnp.dot(a, b, preferred_element_type=f32)


def from_peer(block, axis, count, k):
    return lax.ppermute(block, axis, [(i, i ^ k) for i in range(count)])


def from_peers(blocks, axis, count):
    return [blocks[0]] + [from_peer(blocks[k], axis, count, k) for k in range(1, count)]


def add(blocks):
    total = blocks[0].astype(f32)
    for block in blocks[1:]:
        total = total + block.astype(f32)
    return total


def split(value):
    high = lax.reduce_precision(value, 8, 7)
    return high.astype(bf16), (value - high).astype(bf16)


def gather_column(keys_values, x_index):
    height = keys_values.shape[0] // (NY * NC)
    piece = lax.axis_index(("y", "core"))
    key_piece = lax.dynamic_slice(keys_values, (piece * height, x_index * HD), (height, HD))
    value_piece = lax.dynamic_slice(
        keys_values, (piece * height, (KV_HEADS + x_index) * HD), (height, HD)
    )
    return share(jnp.concatenate([key_piece, value_piece], axis=1), CTX, NCTX)


def key_positions(rows):
    height = rows // (NY * NC)
    number = jnp.arange(NCTX * rows, dtype=jnp.int32)
    return (
        (number % (NCTX * height)) // height * rows
        + number // (NCTX * height) * height
        + number % height
    )


def call(kernel, shape, operands, weights):
    return pl.pallas_call(
        kernel,
        out_shape=jax.ShapeDtypeStruct(shape, bf16),
        in_specs=[pl.BlockSpec(memory_space=pltpu.VMEM)] * len(operands)
        + [pl.BlockSpec(memory_space=pltpu.HBM)] * len(weights),
        out_specs=pl.BlockSpec(memory_space=pltpu.VMEM),
        scratch_shapes=[
            pltpu.VMEM((len(weights),) + weights[0].shape, bf16),
            pltpu.SemaphoreType.DMA((len(weights),)),
        ],
        compiler_params=pltpu.CompilerParams(vmem_limit_bytes=32 * 1024 * 1024),
    )(*operands, *weights)


def fetch(weights, held, semaphores):
    copies = [
        pltpu.make_async_copy(weight, held.at[i], semaphores.at[i])
        for i, weight in enumerate(weights)
    ]
    for copy in copies:
        copy.start()
    return copies


def gate_up_kernel(buffer_ref, gain_ref, *refs):
    *weights, out_ref, held, semaphores = refs
    copies = fetch(weights, held, semaphores)
    _, feat, units = held.shape
    rows = buffer_ref.shape[0] // NP
    buffer = buffer_ref[...].astype(f32)
    squares = jnp.sum(buffer * buffer, axis=1, keepdims=True)
    scaled = (buffer * gain_ref[...]).astype(bf16)
    for half in range(2):
        total = jnp.zeros((buffer.shape[0], units), f32)
        for k in range(NQ):
            copies[half * NQ + k].wait()
            total = total + dot(scaled[:, k * feat : (k + 1) * feat], held[half * NQ + k])
        total = total.astype(bf16)
        for p in range(NP):
            for chunk in range(units // HD):
                start = (half * (units // HD) + chunk) * rows
                out_ref[p, start : start + rows, :] = total[
                    p * rows : (p + 1) * rows, chunk * HD : (chunk + 1) * HD
                ]
    body = 2 * (units // HD) * rows
    lane = lax.broadcasted_iota(jnp.int32, (rows, HD), 1)
    on_diagonal = lane == lax.broadcasted_iota(jnp.int32, (rows, HD), 0)
    row = lax.broadcasted_iota(jnp.int32, (16, HD), 0)
    for p in range(NP):
        column = jnp.broadcast_to(squares[p * rows : (p + 1) * rows], (rows, HD))
        line = jnp.sum(jnp.where(on_diagonal, column, 0.0), axis=0, keepdims=True)
        high = line.astype(bf16).astype(f32)
        pair = jnp.where(row == 0, high, jnp.where(row == 1, line - high, 0.0))
        out_ref[p, body : body + 16, :] = pair.astype(bf16)


def down_kernel(activated_ref, *refs):
    *weights, out_ref, held, semaphores = refs
    copies = fetch(weights, held, semaphores)
    parts, chunks, rows, _ = activated_ref.shape
    feat = held.shape[2]
    activated = jnp.concatenate(
        [
            jnp.concatenate([activated_ref[p, chunk] for chunk in range(chunks)], axis=1)
            for p in range(parts)
        ],
        axis=0,
    )
    for k in range(NQ):
        copies[k].wait()
        out_ref[:, k * feat : (k + 1) * feat] = dot(activated, held[k]).astype(bf16)


def attend(queries, key_part, value_part, key_pos, ctx_index):
    rows = queries.shape[0]
    query_pos = ctx_index * rows + jnp.arange(rows, dtype=jnp.int32)
    scores = (
        jnp.einsum("qd,kd->qk", queries, key_part, preferred_element_type=f32) * HD ** (-0.5)
    )
    allowed = key_pos[None, :] <= query_pos[:, None]
    scores = jnp.where(allowed, scores, masked_score)
    top = jnp.max(scores, axis=-1, keepdims=True)
    weights = jnp.where(allowed, jnp.exp(scores - top), 0.0)
    total = jnp.sum(weights, axis=-1, keepdims=True)
    return (dot(weights.astype(bf16), value_part) / total).astype(bf16)


def shards(
    queries,
    keys_values,
    residual,
    norm_gain,
    out_weight,
    expert_ids,
    gate_values,
    gate_up_weight,
    down_weight,
):
    p_index = lax.axis_index("p")
    q_index = lax.axis_index("q")
    x_index = lax.axis_index("x")
    zh_index = lax.axis_index("zh")
    ctx_index = lax.axis_index(CTX)
    gate_up_weight = gate_up_weight[0]
    down_weight = down_weight[0]
    feat = down_weight.shape[1]
    units = down_weight.shape[0] // NQ
    width = NQ * feat
    model = NP * width

    def gate_block(target):
        return lax.dynamic_slice(gate_up_weight, (0, target * units), (feat, units))

    def up_block(target):
        return lax.dynamic_slice(gate_up_weight, (0, (NQ + target) * units), (feat, units))

    def down_block(target):
        return lax.dynamic_slice(down_weight, (target * units, 0), (units, feat))

    targets = [jnp.bitwise_xor(q_index, k) for k in range(NQ)]
    sent = {
        name: [block(target) for target in targets]
        for name, block in (("gate", gate_block), ("up", up_block), ("down", down_block))
    }
    moved = {(name, 0): blocks[0] for name, blocks in sent.items()}

    def begin(first, *units_sent):
        blocks = [sent[name][k] for name, k in units_sent]
        if first is not None:
            first, blocks = lax.optimization_barrier((first, blocks))
        arriving = [from_peer(block, "q", NQ, k) for block, (_, k) in zip(blocks, units_sent)]
        return first, (units_sent, arriving)

    def end(last, flight):
        units_sent, arriving = flight
        last, arriving = lax.optimization_barrier((last, arriving))
        moved.update(zip(units_sent, arriving))
        return last

    rows = keys_values.shape[0]
    _, flight = begin(None, ("gate", 1), ("up", 1), ("gate", 2))
    column = end(gather_column(keys_values, x_index), flight)
    column, flight = begin(column, ("up", 2))
    segment = end(share(column, ("y", "core"), NY * NC), flight).reshape(NCTX * rows, 2 * HD)
    attended = attend(
        queries, segment[:, :HD], segment[:, HD:], key_positions(rows), ctx_index
    )
    attended, flight = begin(attended, ("gate", 3), ("up", 3))

    share_rows = attended.shape[0] // (NPLANE * NZ)
    attended = (
        attended.reshape(NX, NZ, NY, NC, share_rows, HD)
        .transpose(0, 2, 3, 1, 4, 5)
        .reshape(-1, HD)
    )
    partial = dot(attended, out_weight).astype(bf16).reshape(NPLANE, NZ * share_rows, model)
    partial = end(swap(partial, PLANE), flight)
    partial = jnp.sum(partial.astype(f32), axis=0).reshape(NZ, share_rows, model)
    own_group = jnp.arange(NZ)[:, None, None] == zh_index
    partial = partial + jnp.where(own_group, residual.astype(f32)[None], 0.0)
    outgoing = partial.astype(bf16).reshape(NZ * share_rows, NCTX, feat).transpose(1, 0, 2)

    routing = jnp.concatenate([expert_ids.astype(bf16), *split(gate_values)], axis=1)
    outgoing, routing = lax.optimization_barrier((outgoing, routing))
    other = from_peer(routing, "zh", NZ, 1)
    outgoing, flight = begin(outgoing, ("down", 1), ("down", 2), ("down", 3))
    outgoing = jnp.broadcast_to(
        outgoing[:, None], (NCTX, NZ, NZ * share_rows, feat)
    ).reshape(NCTX * NZ, NZ * share_rows, feat)
    arrived = swap(outgoing, CTX + ("zh",)).reshape(NCTX, NZ, NZ * share_rows, feat)
    arrived, other = lax.optimization_barrier((end(arrived, flight), other))
    hidden = jnp.sum(arrived.astype(f32), axis=1).astype(bf16).reshape(-1, feat)
    choices = expert_ids.shape[1]
    token_count = expert_ids.shape[0]
    first = zh_index == 0
    routing = jnp.stack([jnp.where(first, routing, other), jnp.where(first, other, routing)])
    routing = routing.astype(f32)

    hidden = jnp.concatenate(from_peers([hidden] * NQ, "q", NQ), axis=1)
    gain = jnp.concatenate(
        [
            lax.dynamic_slice_in_dim(
                norm_gain, (p_index * NQ + jnp.bitwise_xor(q_index, k)) * feat, feat, 0
            )
            for k in range(NQ)
        ]
    )

    number = jnp.arange(NPLANE, dtype=jnp.int32)
    experts = (number // (NY * NC) * NZ + zh_index) * (NY * NC) + number % (NY * NC)
    experts = experts.astype(f32)
    slots = NZ * CAP
    total_slots = NPLANE * slots
    tokens = NZ * token_count
    slot_number = jnp.arange(total_slots, dtype=jnp.int32)
    slot_group = slot_number % slots // CAP
    slot_value = (slot_number % CAP).astype(f32)
    owner = (slot_number[None, :] // slots == number[:, None]).astype(bf16)

    def slots_of(table, group, time):
        picked = table[:, :choices, None] == experts
        chosen = jnp.sum(picked.astype(f32), axis=1)
        before = (group[:, None] == group[None, :]) & (time[None, :] < time[:, None])
        slot = dot(before.astype(bf16), chosen.astype(bf16))
        return jnp.where(chosen > 0, slot, -1.0).astype(bf16), picked

    row = jnp.arange(tokens, dtype=jnp.int32)
    group = row // share_rows % NZ
    table = (
        routing.reshape(NZ, NCTX, share_rows, -1).transpose(1, 0, 2, 3).reshape(tokens, -1)
    )
    slot, _ = slots_of(table, group, row)
    slot = lax.dot_general(owner, slot, (((0,), (1,)), ((), ())), preferred_element_type=f32)
    selector = (slot == slot_value[:, None]) & (slot_group[:, None] == group[None, :])
    selector = selector.astype(bf16)

    group = row // token_count
    table = routing.reshape(tokens, -1)
    slot, picked = slots_of(table, group, row)
    taken = (dot(slot, owner) == slot_value[None, :]) & (slot_group[None, :] == group[:, None])
    combine = []
    for part in (1, 2):
        gates = table[:, part * choices : (part + 1) * choices, None]
        gates = jnp.sum(jnp.where(picked, gates, 0.0), axis=1).astype(bf16)
        combine.append(jnp.where(taken, dot(gates, owner), 0.0).astype(bf16))

    buckets = dot(selector, hidden).astype(bf16).reshape(NPLANE, -1, HD)
    buffer = swap(buckets, PLANE).reshape(total_slots, width)

    rows = total_slots // NP
    chunks = 2 * units // HD
    names = [(name, k) for name in ("gate", "up") for k in range(NQ)]
    body = call(
        gate_up_kernel,
        (NP, chunks * rows + 16, HD),
        (buffer, gain[None]),
        [moved[name] for name in names],
    )
    parts = [
        lax.dynamic_index_in_dim(body, jnp.bitwise_xor(p_index, k), 0, keepdims=False)
        for k in range(NP)
    ]
    summed = add(from_peers(parts, "p", NP))
    square_sum = summed[chunks * rows] + summed[chunks * rows + 1]
    scale = lax.rsqrt(square_sum[:rows] / model + 1e-06)
    pre = summed[: chunks * rows].reshape(2, chunks // 2, rows, HD) * scale[:, None]
    activated = (jax.nn.silu(pre[0]) * pre[1]).astype(bf16)
    activated = share(activated, "p", NP)
    expert_out = call(
        down_kernel,
        (total_slots, width),
        (activated.reshape(NP, chunks // 2, rows, HD),),
        [moved["down", k] for k in range(NQ)],
    )
    returned = swap(expert_out.reshape(NPLANE, -1, HD), PLANE).reshape(total_slots, width)
    mixed = dot(combine[0], returned) + dot(combine[1], returned)
    parts = [mixed[:, k * feat : (k + 1) * feat] for k in range(NQ)]
    landed = add(from_peers(parts[:1] + [part.astype(bf16) for part in parts[1:]], "q", NQ))
    landed = landed.reshape(NZ, token_count, feat)
    passed = lax.dynamic_index_in_dim(landed, NZ - 1 - zh_index, 0, keepdims=False)
    passed = from_peer(passed.astype(bf16), "zh", NZ, 1)
    landed = lax.dynamic_index_in_dim(landed, zh_index, 0, keepdims=False) + passed.astype(f32)
    stream = hidden[:, :feat].reshape(NCTX, NZ, share_rows, feat)
    stream = lax.dynamic_index_in_dim(stream, zh_index, 1, keepdims=False)
    return (stream.reshape(token_count, feat).astype(f32) + landed).astype(bf16)


def solution(mesh):
    fine = Mesh(mesh.devices.reshape(NP, NQ, NX, NZ, NY, NC), CTX + EXP)
    in_specs = (
        P(CTX, EXP),
        P(CTX, None),
        P(CTX + EXP, None),
        P(),
        P(EXP, None),
        P(EXP, None),
        P(EXP, None),
        P(EXP, CTX, None),
        P(EXP, None, CTX),
    )
    return jax.shard_map(
        shards, mesh=fine, in_specs=in_specs, out_specs=P(EXP, CTX), check_vma=False
    )
```

```python
import jax
import jax.numpy as jnp
from jax import lax
from jax.experimental import pallas as pl
from jax.experimental.pallas import tpu as pltpu
from jax.sharding import Mesh, PartitionSpec as P

HD = 128
KV_HEADS = 4
CAP = 5

NP, NQ = 4, 4
NX, NZ, NY, NC = 4, 2, 4, 2

CTX = ("p", "q")
EXP = ("x", "zh", "y", "core")
PLANE = ("x", "y", "core")
NPLANE = NX * NY * NC
NCTX = NP * NQ

masked_score = -1e30
f32 = jnp.float32
bf16 = jnp.bfloat16


def swap(array, axes):
    return lax.all_to_all(array, axes, split_axis=0, concat_axis=0, tiled=True)


def share(block, axes, count):
    return swap(jnp.broadcast_to(block[None], (count,) + block.shape), axes)


def dot(a, b):
    return jnp.dot(a, b, preferred_element_type=f32)


def from_peer(block, axis, count, k):
    return lax.ppermute(block, axis, [(i, i ^ k) for i in range(count)])


def from_peers(blocks, axis, count):
    return [blocks[0]] + [from_peer(blocks[k], axis, count, k) for k in range(1, count)]


def add(blocks):
    total = blocks[0].astype(f32)
    for block in blocks[1:]:
        total = total + block.astype(f32)
    return total


def split(value):
    high = lax.reduce_precision(value, 8, 7)
    return high.astype(bf16), (value - high).astype(bf16)


def gather_column(keys_values, x_index):
    height = keys_values.shape[0] // (NY * NC)
    piece = lax.axis_index(("y", "core"))
    key_piece = lax.dynamic_slice(keys_values, (piece * height, x_index * HD), (height, HD))
    value_piece = lax.dynamic_slice(
        keys_values, (piece * height, (KV_HEADS + x_index) * HD), (height, HD)
    )
    return share(jnp.concatenate([key_piece, value_piece], axis=1), CTX, NCTX)


def key_positions(rows):
    height = rows // (NY * NC)
    number = jnp.arange(NCTX * rows, dtype=jnp.int32)
    return (
        (number % (NCTX * height)) // height * rows
        + number // (NCTX * height) * height
        + number % height
    )


def call(kernel, shape, operands, weights):
    return pl.pallas_call(
        kernel,
        out_shape=jax.ShapeDtypeStruct(shape, bf16),
        in_specs=[pl.BlockSpec(memory_space=pltpu.VMEM)] * len(operands)
        + [pl.BlockSpec(memory_space=pltpu.HBM)] * len(weights),
        out_specs=pl.BlockSpec(memory_space=pltpu.VMEM),
        scratch_shapes=[
            pltpu.VMEM((len(weights),) + weights[0].shape, bf16),
            pltpu.SemaphoreType.DMA((len(weights),)),
        ],
        compiler_params=pltpu.CompilerParams(vmem_limit_bytes=32 * 1024 * 1024),
    )(*operands, *weights)


def fetch(weights, held, semaphores):
    copies = [
        pltpu.make_async_copy(weight, held.at[i], semaphores.at[i])
        for i, weight in enumerate(weights)
    ]
    for copy in copies:
        copy.start()
    return copies


def gate_up_kernel(buffer_ref, gain_ref, *refs):
    *weights, out_ref, held, semaphores = refs
    copies = fetch(weights, held, semaphores)
    units = held.shape[2]
    rows = buffer_ref.shape[0] // NP
    buffer = buffer_ref[...].astype(f32)
    squares = jnp.sum(buffer * buffer, axis=1, keepdims=True)
    scaled = (buffer * gain_ref[...]).astype(bf16)
    for half in range(2):
        copies[half].wait()
        total = dot(scaled, held[half]).astype(bf16)
        for p in range(NP):
            for chunk in range(units // HD):
                start = (half * (units // HD) + chunk) * rows
                out_ref[p, start : start + rows, :] = total[
                    p * rows : (p + 1) * rows, chunk * HD : (chunk + 1) * HD
                ]
    body = 2 * (units // HD) * rows
    lane = lax.broadcasted_iota(jnp.int32, (rows, HD), 1)
    on_diagonal = lane == lax.broadcasted_iota(jnp.int32, (rows, HD), 0)
    row = lax.broadcasted_iota(jnp.int32, (16, HD), 0)
    for p in range(NP):
        column = jnp.broadcast_to(squares[p * rows : (p + 1) * rows], (rows, HD))
        line = jnp.sum(jnp.where(on_diagonal, column, 0.0), axis=0, keepdims=True)
        high = line.astype(bf16).astype(f32)
        pair = jnp.where(row == 0, high, jnp.where(row == 1, line - high, 0.0))
        out_ref[p, body : body + 16, :] = pair.astype(bf16)


def down_kernel(activated_ref, *refs):
    *weights, out_ref, held, semaphores = refs
    copies = fetch(weights, held, semaphores)
    parts, chunks, rows, _ = activated_ref.shape
    feat = held.shape[2]
    activated = jnp.concatenate(
        [
            jnp.concatenate([activated_ref[p, chunk] for chunk in range(chunks)], axis=1)
            for p in range(parts)
        ],
        axis=0,
    )
    for k in range(NQ):
        copies[k].wait()
        out_ref[:, k * feat : (k + 1) * feat] = dot(activated, held[k]).astype(bf16)


def attend(queries, key_part, value_part, key_pos, ctx_index):
    rows = queries.shape[0]
    query_pos = ctx_index * rows + jnp.arange(rows, dtype=jnp.int32)
    scores = (
        jnp.einsum("qd,kd->qk", queries, key_part, preferred_element_type=f32) * HD ** (-0.5)
    )
    allowed = key_pos[None, :] <= query_pos[:, None]
    scores = jnp.where(allowed, scores, masked_score)
    top = jnp.max(scores, axis=-1, keepdims=True)
    weights = jnp.where(allowed, jnp.exp(scores - top), 0.0)
    total = jnp.sum(weights, axis=-1, keepdims=True)
    return (dot(weights.astype(bf16), value_part) / total).astype(bf16)


def shards(
    queries,
    keys_values,
    residual,
    norm_gain,
    out_weight,
    expert_ids,
    gate_values,
    gate_up_weight,
    down_weight,
):
    p_index = lax.axis_index("p")
    q_index = lax.axis_index("q")
    x_index = lax.axis_index("x")
    zh_index = lax.axis_index("zh")
    ctx_index = lax.axis_index(CTX)
    gate_up_weight = gate_up_weight[0]
    down_weight = down_weight[0]
    feat = down_weight.shape[1]
    units = down_weight.shape[0] // NQ
    width = NQ * feat
    model = NP * width

    def gate_block(target):
        return lax.dynamic_slice(gate_up_weight, (0, target * units), (feat, units))

    def up_block(target):
        return lax.dynamic_slice(gate_up_weight, (0, (NQ + target) * units), (feat, units))

    def down_block(target):
        return lax.dynamic_slice(down_weight, (target * units, 0), (units, feat))

    targets = [jnp.bitwise_xor(q_index, k) for k in range(NQ)]
    sent = {
        name: [block(target) for target in targets]
        for name, block in (("gate", gate_block), ("up", up_block), ("down", down_block))
    }
    moved = {(name, 0): blocks[0] for name, blocks in sent.items()}

    def begin(first, *units_sent):
        blocks = [sent[name][k] for name, k in units_sent]
        if first is not None:
            first, blocks = lax.optimization_barrier((first, blocks))
        arriving = [from_peer(block, "q", NQ, k) for block, (_, k) in zip(blocks, units_sent)]
        return first, (units_sent, arriving)

    def end(last, flight):
        units_sent, arriving = flight
        last, arriving = lax.optimization_barrier((last, arriving))
        moved.update(zip(units_sent, arriving))
        return last

    rows = keys_values.shape[0]
    _, flight = begin(None, ("gate", 1), ("up", 1), ("gate", 2))
    column = end(gather_column(keys_values, x_index), flight)
    column, flight = begin(column, ("up", 2))
    segment = end(share(column, ("y", "core"), NY * NC), flight).reshape(NCTX * rows, 2 * HD)
    attended = attend(
        queries, segment[:, :HD], segment[:, HD:], key_positions(rows), ctx_index
    )
    attended, flight = begin(attended, ("gate", 3), ("up", 3))

    share_rows = attended.shape[0] // (NPLANE * NZ)
    attended = (
        attended.reshape(NX, NZ, NY, NC, share_rows, HD)
        .transpose(0, 2, 3, 1, 4, 5)
        .reshape(-1, HD)
    )
    partial = dot(attended, out_weight).astype(bf16).reshape(NPLANE, NZ * share_rows, model)
    partial = end(swap(partial, PLANE), flight)
    partial = jnp.sum(partial.astype(f32), axis=0).reshape(NZ, share_rows, model)
    own_group = jnp.arange(NZ)[:, None, None] == zh_index
    partial = partial + jnp.where(own_group, residual.astype(f32)[None], 0.0)
    outgoing = partial.astype(bf16).reshape(NZ * share_rows, NCTX, feat).transpose(1, 0, 2)

    routing = jnp.concatenate([expert_ids.astype(bf16), *split(gate_values)], axis=1)
    fields = routing.shape[1]
    routing = lax.dynamic_slice_in_dim(routing, ctx_index * share_rows, share_rows, 0)
    routing = jnp.pad(routing, ((0, 0), (0, HD - fields)))
    routing = jnp.where(own_group, routing[None], 0).reshape(1, NZ * share_rows, HD)
    routing = jnp.broadcast_to(routing, (NCTX,) + routing.shape[1:])
    outgoing = jnp.concatenate([outgoing, routing], axis=2)
    outgoing, flight = begin(outgoing, ("down", 1), ("down", 2))
    wide = feat + HD
    outgoing = jnp.broadcast_to(
        outgoing[:, None], (NCTX, NZ, NZ * share_rows, wide)
    ).reshape(NCTX * NZ, NZ * share_rows, wide)
    arrived = swap(outgoing, CTX + ("zh",)).reshape(NCTX, NZ, NZ * share_rows, wide)
    weight_in = [
        jnp.concatenate([moved[name, k] for k in range(NQ)], axis=0) for name in ("gate", "up")
    ]
    arrived, weight_in = lax.optimization_barrier((end(arrived, flight), weight_in))
    arrived = jnp.sum(arrived.astype(f32), axis=1)
    hidden = arrived[:, :, :feat].astype(bf16).reshape(-1, feat)
    routing = arrived[:, :, feat : feat + fields].reshape(-1, fields)
    choices = expert_ids.shape[1]
    token_count = expert_ids.shape[0]

    hidden = jnp.concatenate(from_peers([hidden] * NQ, "q", NQ), axis=1)
    gain = jnp.concatenate(
        [
            lax.dynamic_slice_in_dim(
                norm_gain, (p_index * NQ + jnp.bitwise_xor(q_index, k)) * feat, feat, 0
            )
            for k in range(NQ)
        ]
    )

    number = jnp.arange(NPLANE, dtype=jnp.int32)
    experts = (number // (NY * NC) * NZ + zh_index) * (NY * NC) + number % (NY * NC)
    experts = experts.astype(f32)
    slots = NZ * CAP
    total_slots = NPLANE * slots
    tokens = NZ * token_count
    slot_number = jnp.arange(total_slots, dtype=jnp.int32)
    slot_group = slot_number % slots // CAP
    slot_value = (slot_number % CAP).astype(f32)
    owner = (slot_number[None, :] // slots == number[:, None]).astype(bf16)

    def slots_of(table, group, time):
        picked = table[:, :choices, None] == experts
        chosen = jnp.sum(picked.astype(f32), axis=1)
        before = (group[:, None] == group[None, :]) & (time[None, :] < time[:, None])
        slot = dot(before.astype(bf16), chosen.astype(bf16))
        return jnp.where(chosen > 0, slot, -1.0).astype(bf16), picked

    row = jnp.arange(tokens, dtype=jnp.int32)
    group = row // share_rows % NZ
    table = routing
    slot, _ = slots_of(table, group, row)
    slot = lax.dot_general(owner, slot, (((0,), (1,)), ((), ())), preferred_element_type=f32)
    selector = (slot == slot_value[:, None]) & (slot_group[:, None] == group[None, :])
    selector = selector.astype(bf16)

    group = row // token_count
    table = (
        routing.reshape(NCTX, NZ, share_rows, -1).transpose(1, 0, 2, 3).reshape(tokens, -1)
    )
    slot, picked = slots_of(table, group, row)
    taken = (dot(slot, owner) == slot_value[None, :]) & (slot_group[None, :] == group[:, None])
    combine = []
    for part in (1, 2):
        gates = table[:, part * choices : (part + 1) * choices, None]
        gates = jnp.sum(jnp.where(picked, gates, 0.0), axis=1).astype(bf16)
        combine.append(jnp.where(taken, dot(gates, owner), 0.0).astype(bf16))

    buckets = dot(selector, hidden).astype(bf16).reshape(NPLANE, -1, HD)
    buckets, flight = begin(buckets, ("down", 3))
    buffer = end(swap(buckets, PLANE), flight).reshape(total_slots, width)

    rows = total_slots // NP
    chunks = 2 * units // HD
    body = call(
        gate_up_kernel,
        (NP, chunks * rows + 16, HD),
        (buffer, gain[None]),
        weight_in,
    )
    parts = [
        lax.dynamic_index_in_dim(body, jnp.bitwise_xor(p_index, k), 0, keepdims=False)
        for k in range(NP)
    ]
    summed = add(from_peers(parts, "p", NP))
    square_sum = summed[chunks * rows] + summed[chunks * rows + 1]
    scale = lax.rsqrt(square_sum[:rows] / model + 1e-06)
    pre = summed[: chunks * rows].reshape(2, chunks // 2, rows, HD) * scale[:, None]
    activated = (jax.nn.silu(pre[0]) * pre[1]).astype(bf16)
    activated = share(activated, "p", NP)
    expert_out = call(
        down_kernel,
        (total_slots, width),
        (activated.reshape(NP, chunks // 2, rows, HD),),
        [moved["down", k] for k in range(NQ)],
    )
    returned = swap(expert_out.reshape(NPLANE, -1, HD), PLANE).reshape(total_slots, width)
    mixed = dot(combine[0], returned) + dot(combine[1], returned)
    parts = [mixed[:, k * feat : (k + 1) * feat] for k in range(NQ)]
    landed = add(from_peers(parts[:1] + [part.astype(bf16) for part in parts[1:]], "q", NQ))
    landed = landed.reshape(NZ, token_count, feat)
    passed = lax.dynamic_index_in_dim(landed, NZ - 1 - zh_index, 0, keepdims=False)
    passed = from_peer(passed.astype(bf16), "zh", NZ, 1)
    landed = lax.dynamic_index_in_dim(landed, zh_index, 0, keepdims=False) + passed.astype(f32)
    stream = hidden[:, :feat].reshape(NCTX, NZ, share_rows, feat)
    stream = lax.dynamic_index_in_dim(stream, zh_index, 1, keepdims=False)
    return (stream.reshape(token_count, feat).astype(f32) + landed).astype(bf16)


def solution(mesh):
    fine = Mesh(mesh.devices.reshape(NP, NQ, NX, NZ, NY, NC), CTX + EXP)
    in_specs = (
        P(CTX, EXP),
        P(CTX, None),
        P(CTX + EXP, None),
        P(),
        P(EXP, None),
        P(EXP, None),
        P(EXP, None),
        P(EXP, CTX, None),
        P(EXP, None, CTX),
    )
    return jax.shard_map(
        shards, mesh=fine, in_specs=in_specs, out_specs=P(EXP, CTX), check_vma=False
    )
```

```python
import jax
import jax.numpy as jnp
from jax import lax
from jax.experimental import pallas as pl
from jax.experimental.pallas import tpu as pltpu
from jax.sharding import Mesh, PartitionSpec as P

HD = 128
KV_HEADS = 4
CAP = 5

NP, NQ = 4, 4
NX, NZ, NY, NC = 4, 2, 4, 2

CTX = ("p", "q")
EXP = ("x", "zh", "y", "core")
PLANE = ("x", "y", "core")
NPLANE = NX * NY * NC
NCTX = NP * NQ

masked_score = -1e30
f32 = jnp.float32
bf16 = jnp.bfloat16


def swap(array, axes):
    return lax.all_to_all(array, axes, split_axis=0, concat_axis=0, tiled=True)


def share(block, axes, count):
    return swap(jnp.broadcast_to(block[None], (count,) + block.shape), axes)


def dot(a, b):
    return jnp.dot(a, b, preferred_element_type=f32)


def from_peer(block, axis, count, k):
    return lax.ppermute(block, axis, [(i, i ^ k) for i in range(count)])


def from_peers(blocks, axis, count):
    return [blocks[0]] + [from_peer(blocks[k], axis, count, k) for k in range(1, count)]


def add(blocks):
    total = blocks[0].astype(f32)
    for block in blocks[1:]:
        total = total + block.astype(f32)
    return total


def split(value):
    high = lax.reduce_precision(value, 8, 7)
    return high.astype(bf16), (value - high).astype(bf16)


def gather_column(keys_values, x_index):
    height = keys_values.shape[0] // (NY * NC)
    piece = lax.axis_index(("y", "core"))
    key_piece = lax.dynamic_slice(keys_values, (piece * height, x_index * HD), (height, HD))
    value_piece = lax.dynamic_slice(
        keys_values, (piece * height, (KV_HEADS + x_index) * HD), (height, HD)
    )
    return share(jnp.concatenate([key_piece, value_piece], axis=1), CTX, NCTX)


def call(kernel, shape, operands, weights):
    return pl.pallas_call(
        kernel,
        out_shape=jax.ShapeDtypeStruct(shape, bf16),
        in_specs=[pl.BlockSpec(memory_space=pltpu.VMEM)] * len(operands)
        + [pl.BlockSpec(memory_space=pltpu.HBM)] * len(weights),
        out_specs=pl.BlockSpec(memory_space=pltpu.VMEM),
        scratch_shapes=[
            pltpu.VMEM((len(weights),) + weights[0].shape, bf16),
            pltpu.SemaphoreType.DMA((len(weights),)),
        ],
        compiler_params=pltpu.CompilerParams(vmem_limit_bytes=32 * 1024 * 1024),
    )(*operands, *weights)


def fetch(weights, held, semaphores):
    copies = [
        pltpu.make_async_copy(weight, held.at[i], semaphores.at[i])
        for i, weight in enumerate(weights)
    ]
    for copy in copies:
        copy.start()
    return copies


def gate_up_kernel(buffer_ref, gain_ref, *refs):
    *weights, out_ref, held, semaphores = refs
    copies = fetch(weights, held, semaphores)
    units = held.shape[2]
    rows = buffer_ref.shape[0] // NP
    buffer = buffer_ref[...].astype(f32)
    squares = jnp.sum(buffer * buffer, axis=1, keepdims=True)
    scaled = (buffer * gain_ref[...]).astype(bf16)
    for half in range(2):
        copies[half].wait()
        total = dot(scaled, held[half]).astype(bf16)
        for p in range(NP):
            for chunk in range(units // HD):
                start = (half * (units // HD) + chunk) * rows
                out_ref[p, start : start + rows, :] = total[
                    p * rows : (p + 1) * rows, chunk * HD : (chunk + 1) * HD
                ]
    body = 2 * (units // HD) * rows
    lane = lax.broadcasted_iota(jnp.int32, (rows, HD), 1)
    on_diagonal = lane == lax.broadcasted_iota(jnp.int32, (rows, HD), 0)
    row = lax.broadcasted_iota(jnp.int32, (16, HD), 0)
    for p in range(NP):
        column = jnp.broadcast_to(squares[p * rows : (p + 1) * rows], (rows, HD))
        line = jnp.sum(jnp.where(on_diagonal, column, 0.0), axis=0, keepdims=True)
        high = line.astype(bf16).astype(f32)
        pair = jnp.where(row == 0, high, jnp.where(row == 1, line - high, 0.0))
        out_ref[p, body : body + 16, :] = pair.astype(bf16)


def down_kernel(activated_ref, *refs):
    *weights, out_ref, held, semaphores = refs
    copies = fetch(weights, held, semaphores)
    parts, chunks, rows, _ = activated_ref.shape
    feat = held.shape[2]
    activated = jnp.concatenate(
        [
            jnp.concatenate([activated_ref[p, chunk] for chunk in range(chunks)], axis=1)
            for p in range(parts)
        ],
        axis=0,
    )
    for k in range(NQ):
        copies[k].wait()
        out_ref[:, k * feat : (k + 1) * feat] = dot(activated, held[k]).astype(bf16)


def attend_column(queries, column, ctx_index):
    heads, rows, _ = queries.shape
    height = column.shape[1]
    piece = lax.axis_index(("y", "core"))
    keys = column.reshape(-1, 2 * HD)
    number = jnp.arange(keys.shape[0], dtype=jnp.int32)
    key_pos = number // height * rows + piece * height + number % height
    query_pos = ctx_index * rows + jnp.arange(rows, dtype=jnp.int32)
    allowed = key_pos[None, None, :] <= query_pos[None, :, None]
    scores = (
        jnp.einsum("hqd,kd->hqk", queries, keys[:, :HD], preferred_element_type=f32)
        * HD ** (-0.5)
    )
    scores = jnp.where(allowed, scores, masked_score)
    shift = lax.reduce_precision(jnp.max(scores, axis=-1), 8, 7)
    weights = jnp.where(allowed, jnp.exp(scores - shift[:, :, None]), 0.0)
    total = jnp.sum(weights, axis=-1)
    sums = jnp.einsum(
        "hqk,kd->hqd", weights.astype(bf16), keys[:, HD:], preferred_element_type=f32
    )
    stats = jnp.stack([shift.astype(bf16), *split(total)], axis=1)
    stats = jnp.pad(stats, ((0, 0), (0, 16 - stats.shape[1]), (0, HD - rows)))
    return jnp.concatenate([sums.astype(bf16), stats], axis=1)


def merge(parts, rows):
    parts = parts.astype(f32)
    shift = parts[:, rows, :rows]
    total = parts[:, rows + 1, :rows] + parts[:, rows + 2, :rows]
    scale = jnp.exp(shift - jnp.max(shift, axis=0, keepdims=True))
    sums = jnp.sum(parts[:, :rows] * scale[:, :, None], axis=0)
    return (sums / jnp.sum(total * scale, axis=0)[:, None]).astype(bf16)


def shards(
    queries,
    keys_values,
    residual,
    norm_gain,
    out_weight,
    expert_ids,
    gate_values,
    gate_up_weight,
    down_weight,
):
    p_index = lax.axis_index("p")
    q_index = lax.axis_index("q")
    x_index = lax.axis_index("x")
    zh_index = lax.axis_index("zh")
    ctx_index = lax.axis_index(CTX)
    gate_up_weight = gate_up_weight[0]
    down_weight = down_weight[0]
    feat = down_weight.shape[1]
    units = down_weight.shape[0] // NQ
    width = NQ * feat
    model = NP * width

    def gate_block(target):
        return lax.dynamic_slice(gate_up_weight, (0, target * units), (feat, units))

    def up_block(target):
        return lax.dynamic_slice(gate_up_weight, (0, (NQ + target) * units), (feat, units))

    def down_block(target):
        return lax.dynamic_slice(down_weight, (target * units, 0), (units, feat))

    targets = [jnp.bitwise_xor(q_index, k) for k in range(NQ)]
    sent = {
        name: [block(target) for target in targets]
        for name, block in (("gate", gate_block), ("up", up_block), ("down", down_block))
    }
    moved = {(name, 0): blocks[0] for name, blocks in sent.items()}

    def begin(first, *units_sent):
        blocks = [sent[name][k] for name, k in units_sent]
        if first is not None:
            first, blocks = lax.optimization_barrier((first, blocks))
        arriving = [from_peer(block, "q", NQ, k) for block, (_, k) in zip(blocks, units_sent)]
        return first, (units_sent, arriving)

    def end(last, flight):
        units_sent, arriving = flight
        last, arriving = lax.optimization_barrier((last, arriving))
        moved.update(zip(units_sent, arriving))
        return last

    rows = keys_values.shape[0]
    _, flight = begin(None, ("gate", 1), ("up", 1), ("gate", 2))
    peers = share(queries, ("y", "core"), NY * NC)
    column = end(gather_column(keys_values, x_index), flight)
    column, peers = lax.optimization_barrier((column, peers))
    attended, flight = begin(attend_column(peers, column, ctx_index), ("up", 2))
    attended = merge(end(swap(attended, ("y", "core")), flight), rows)
    attended, flight = begin(attended, ("gate", 3), ("up", 3))

    share_rows = attended.shape[0] // (NPLANE * NZ)
    attended = (
        attended.reshape(NX, NZ, NY, NC, share_rows, HD)
        .transpose(0, 2, 3, 1, 4, 5)
        .reshape(-1, HD)
    )
    partial = dot(attended, out_weight).astype(bf16).reshape(NPLANE, NZ * share_rows, model)
    partial = end(swap(partial, PLANE), flight)
    partial = jnp.sum(partial.astype(f32), axis=0).reshape(NZ, share_rows, model)
    own_group = jnp.arange(NZ)[:, None, None] == zh_index
    partial = partial + jnp.where(own_group, residual.astype(f32)[None], 0.0)
    outgoing = partial.astype(bf16).reshape(NZ * share_rows, NCTX, feat).transpose(1, 0, 2)

    routing = jnp.concatenate([expert_ids.astype(bf16), *split(gate_values)], axis=1)
    fields = routing.shape[1]
    routing = lax.dynamic_slice_in_dim(routing, ctx_index * share_rows, share_rows, 0)
    routing = jnp.pad(routing, ((0, 0), (0, HD - fields)))
    routing = jnp.where(own_group, routing[None], 0).reshape(1, NZ * share_rows, HD)
    routing = jnp.broadcast_to(routing, (NCTX,) + routing.shape[1:])
    outgoing = jnp.concatenate([outgoing, routing], axis=2)
    outgoing, flight = begin(outgoing, ("down", 1), ("down", 2))
    wide = feat + HD
    outgoing = jnp.broadcast_to(
        outgoing[:, None], (NCTX, NZ, NZ * share_rows, wide)
    ).reshape(NCTX * NZ, NZ * share_rows, wide)
    arrived = swap(outgoing, CTX + ("zh",)).reshape(NCTX, NZ, NZ * share_rows, wide)
    weight_in = [
        jnp.concatenate([moved[name, k] for k in range(NQ)], axis=0) for name in ("gate", "up")
    ]
    arrived, weight_in = lax.optimization_barrier((end(arrived, flight), weight_in))
    arrived = jnp.sum(arrived.astype(f32), axis=1)
    hidden = arrived[:, :, :feat].astype(bf16).reshape(-1, feat)
    routing = arrived[:, :, feat : feat + fields].reshape(-1, fields)
    choices = expert_ids.shape[1]
    token_count = expert_ids.shape[0]

    hidden = jnp.concatenate(from_peers([hidden] * NQ, "q", NQ), axis=1)
    gain = jnp.concatenate(
        [
            lax.dynamic_slice_in_dim(
                norm_gain, (p_index * NQ + jnp.bitwise_xor(q_index, k)) * feat, feat, 0
            )
            for k in range(NQ)
        ]
    )

    number = jnp.arange(NPLANE, dtype=jnp.int32)
    experts = (number // (NY * NC) * NZ + zh_index) * (NY * NC) + number % (NY * NC)
    experts = experts.astype(f32)
    slots = NZ * CAP
    total_slots = NPLANE * slots
    tokens = NZ * token_count
    slot_number = jnp.arange(total_slots, dtype=jnp.int32)
    slot_group = slot_number % slots // CAP
    slot_value = (slot_number % CAP).astype(f32)
    owner = (slot_number[None, :] // slots == number[:, None]).astype(bf16)

    def slots_of(table, group, time):
        picked = table[:, :choices, None] == experts
        chosen = jnp.sum(picked.astype(f32), axis=1)
        before = (group[:, None] == group[None, :]) & (time[None, :] < time[:, None])
        slot = dot(before.astype(bf16), chosen.astype(bf16))
        return jnp.where(chosen > 0, slot, -1.0).astype(bf16), picked

    row = jnp.arange(tokens, dtype=jnp.int32)
    group = row // share_rows % NZ
    table = routing
    slot, _ = slots_of(table, group, row)
    slot = lax.dot_general(owner, slot, (((0,), (1,)), ((), ())), preferred_element_type=f32)
    selector = (slot == slot_value[:, None]) & (slot_group[:, None] == group[None, :])
    selector = selector.astype(bf16)

    group = row // token_count
    table = (
        routing.reshape(NCTX, NZ, share_rows, -1).transpose(1, 0, 2, 3).reshape(tokens, -1)
    )
    slot, picked = slots_of(table, group, row)
    taken = (dot(slot, owner) == slot_value[None, :]) & (slot_group[None, :] == group[:, None])
    combine = []
    for part in (1, 2):
        gates = table[:, part * choices : (part + 1) * choices, None]
        gates = jnp.sum(jnp.where(picked, gates, 0.0), axis=1).astype(bf16)
        combine.append(jnp.where(taken, dot(gates, owner), 0.0).astype(bf16))

    buckets = dot(selector, hidden).astype(bf16).reshape(NPLANE, -1, HD)
    buckets, flight = begin(buckets, ("down", 3))
    buffer = end(swap(buckets, PLANE), flight).reshape(total_slots, width)

    rows = total_slots // NP
    chunks = 2 * units // HD
    body = call(
        gate_up_kernel,
        (NP, chunks * rows + 16, HD),
        (buffer, gain[None]),
        weight_in,
    )
    parts = [
        lax.dynamic_index_in_dim(body, jnp.bitwise_xor(p_index, k), 0, keepdims=False)
        for k in range(NP)
    ]
    summed = add(from_peers(parts, "p", NP))
    square_sum = summed[chunks * rows] + summed[chunks * rows + 1]
    scale = lax.rsqrt(square_sum[:rows] / model + 1e-06)
    pre = summed[: chunks * rows].reshape(2, chunks // 2, rows, HD) * scale[:, None]
    activated = (jax.nn.silu(pre[0]) * pre[1]).astype(bf16)
    activated = share(activated, "p", NP)
    expert_out = call(
        down_kernel,
        (total_slots, width),
        (activated.reshape(NP, chunks // 2, rows, HD),),
        [moved["down", k] for k in range(NQ)],
    )
    returned = swap(expert_out.reshape(NPLANE, -1, HD), PLANE).reshape(total_slots, width)
    mixed = dot(combine[0], returned) + dot(combine[1], returned)
    parts = [mixed[:, k * feat : (k + 1) * feat] for k in range(NQ)]
    landed = add(from_peers(parts[:1] + [part.astype(bf16) for part in parts[1:]], "q", NQ))
    landed = landed.reshape(NZ, token_count, feat)
    passed = lax.dynamic_index_in_dim(landed, NZ - 1 - zh_index, 0, keepdims=False)
    passed = from_peer(passed.astype(bf16), "zh", NZ, 1)
    landed = lax.dynamic_index_in_dim(landed, zh_index, 0, keepdims=False) + passed.astype(f32)
    stream = hidden[:, :feat].reshape(NCTX, NZ, share_rows, feat)
    stream = lax.dynamic_index_in_dim(stream, zh_index, 1, keepdims=False)
    return (stream.reshape(token_count, feat).astype(f32) + landed).astype(bf16)


def solution(mesh):
    fine = Mesh(mesh.devices.reshape(NP, NQ, NX, NZ, NY, NC), CTX + EXP)
    in_specs = (
        P(CTX, EXP),
        P(CTX, None),
        P(CTX + EXP, None),
        P(),
        P(EXP, None),
        P(EXP, None),
        P(EXP, None),
        P(EXP, CTX, None),
        P(EXP, None, CTX),
    )
    return jax.shard_map(
        shards, mesh=fine, in_specs=in_specs, out_specs=P(EXP, CTX), check_vma=False
    )
```

```python
import jax
import jax.numpy as jnp
from jax import lax
from jax.experimental import pallas as pl
from jax.experimental.pallas import tpu as pltpu
from jax.sharding import Mesh, PartitionSpec as P

HD = 128
KV_HEADS = 4
CAP = 5

NP, NQ = 4, 4
NX, NZ, NY, NC = 4, 2, 4, 2

CTX = ("p", "q")
EXP = ("x", "zh", "y", "core")
PLANE = ("x", "y", "core")
NPLANE = NX * NY * NC
NCTX = NP * NQ

masked_score = -1e30
f32 = jnp.float32
bf16 = jnp.bfloat16


def swap(array, axes):
    return lax.all_to_all(array, axes, split_axis=0, concat_axis=0, tiled=True)


def share(block, axes, count):
    return swap(jnp.broadcast_to(block[None], (count,) + block.shape), axes)


def dot(a, b):
    return jnp.dot(a, b, preferred_element_type=f32)


def from_peer(block, axis, count, k):
    return lax.ppermute(block, axis, [(i, i ^ k) for i in range(count)])


def from_peers(blocks, axis, count):
    return [blocks[0]] + [from_peer(blocks[k], axis, count, k) for k in range(1, count)]


def add(blocks):
    total = blocks[0].astype(f32)
    for block in blocks[1:]:
        total = total + block.astype(f32)
    return total


def split(value):
    high = lax.reduce_precision(value, 8, 7)
    return high.astype(bf16), (value - high).astype(bf16)


def gather_column(keys_values, x_index):
    height = keys_values.shape[0] // (NY * NC)
    piece = lax.axis_index(("y", "core"))
    key_piece = lax.dynamic_slice(keys_values, (piece * height, x_index * HD), (height, HD))
    value_piece = lax.dynamic_slice(
        keys_values, (piece * height, (KV_HEADS + x_index) * HD), (height, HD)
    )
    return share(jnp.concatenate([key_piece, value_piece], axis=1), CTX, NCTX)


def key_positions(rows):
    height = rows // (NY * NC)
    number = jnp.arange(NCTX * rows, dtype=jnp.int32)
    return (
        (number % (NCTX * height)) // height * rows
        + number // (NCTX * height) * height
        + number % height
    )


def call(kernel, shape, operands, weights):
    return pl.pallas_call(
        kernel,
        out_shape=jax.ShapeDtypeStruct(shape, bf16),
        in_specs=[pl.BlockSpec(memory_space=pltpu.VMEM)] * len(operands)
        + [pl.BlockSpec(memory_space=pltpu.HBM)] * len(weights),
        out_specs=pl.BlockSpec(memory_space=pltpu.VMEM),
        scratch_shapes=[
            pltpu.VMEM((len(weights),) + weights[0].shape, bf16),
            pltpu.SemaphoreType.DMA((len(weights),)),
        ],
        compiler_params=pltpu.CompilerParams(vmem_limit_bytes=32 * 1024 * 1024),
    )(*operands, *weights)


def fetch(weights, held, semaphores):
    copies = [
        pltpu.make_async_copy(weight, held.at[i], semaphores.at[i])
        for i, weight in enumerate(weights)
    ]
    for copy in copies:
        copy.start()
    return copies


def gate_up_kernel(buffer_ref, gain_ref, *refs):
    *weights, out_ref, held, semaphores = refs
    copies = fetch(weights, held, semaphores)
    units = held.shape[2]
    rows = buffer_ref.shape[0] // NP
    buffer = buffer_ref[...].astype(f32)
    squares = jnp.sum(buffer * buffer, axis=1, keepdims=True)
    scaled = (buffer * gain_ref[...]).astype(bf16)
    for half in range(2):
        copies[half].wait()
        total = dot(scaled, held[half]).astype(bf16)
        for p in range(NP):
            for chunk in range(units // HD):
                start = (half * (units // HD) + chunk) * rows
                out_ref[p, start : start + rows, :] = total[
                    p * rows : (p + 1) * rows, chunk * HD : (chunk + 1) * HD
                ]
    body = 2 * (units // HD) * rows
    lane = lax.broadcasted_iota(jnp.int32, (rows, HD), 1)
    on_diagonal = lane == lax.broadcasted_iota(jnp.int32, (rows, HD), 0)
    row = lax.broadcasted_iota(jnp.int32, (16, HD), 0)
    for p in range(NP):
        column = jnp.broadcast_to(squares[p * rows : (p + 1) * rows], (rows, HD))
        line = jnp.sum(jnp.where(on_diagonal, column, 0.0), axis=0, keepdims=True)
        high = line.astype(bf16).astype(f32)
        pair = jnp.where(row == 0, high, jnp.where(row == 1, line - high, 0.0))
        out_ref[p, body : body + 16, :] = pair.astype(bf16)


def down_kernel(activated_ref, *refs):
    *weights, out_ref, held, semaphores = refs
    copies = fetch(weights, held, semaphores)
    parts, chunks, rows, _ = activated_ref.shape
    feat = held.shape[2]
    activated = jnp.concatenate(
        [
            jnp.concatenate([activated_ref[p, chunk] for chunk in range(chunks)], axis=1)
            for p in range(parts)
        ],
        axis=0,
    )
    for k in range(NQ):
        copies[k].wait()
        out_ref[:, k * feat : (k + 1) * feat] = dot(activated, held[k]).astype(bf16)


def attend(queries, key_part, value_part, key_pos, ctx_index):
    rows = queries.shape[0]
    query_pos = ctx_index * rows + jnp.arange(rows, dtype=jnp.int32)
    scores = (
        jnp.einsum("qd,kd->qk", queries, key_part, preferred_element_type=f32) * HD ** (-0.5)
    )
    allowed = key_pos[None, :] <= query_pos[:, None]
    scores = jnp.where(allowed, scores, masked_score)
    top = jnp.max(scores, axis=-1, keepdims=True)
    weights = jnp.where(allowed, jnp.exp(scores - top), 0.0)
    total = jnp.sum(weights, axis=-1, keepdims=True)
    return (dot(weights.astype(bf16), value_part) / total).astype(bf16)


def shards(
    queries,
    keys_values,
    residual,
    norm_gain,
    out_weight,
    expert_ids,
    gate_values,
    gate_up_weight,
    down_weight,
):
    p_index = lax.axis_index("p")
    q_index = lax.axis_index("q")
    x_index = lax.axis_index("x")
    zh_index = lax.axis_index("zh")
    ctx_index = lax.axis_index(CTX)
    gate_up_weight = gate_up_weight[0]
    down_weight = down_weight[0]
    feat = down_weight.shape[1]
    units = down_weight.shape[0] // NQ
    width = NQ * feat
    model = NP * width

    def gate_block(target):
        return lax.dynamic_slice(gate_up_weight, (0, target * units), (feat, units))

    def up_block(target):
        return lax.dynamic_slice(gate_up_weight, (0, (NQ + target) * units), (feat, units))

    def down_block(target):
        return lax.dynamic_slice(down_weight, (target * units, 0), (units, feat))

    targets = [jnp.bitwise_xor(q_index, k) for k in range(NQ)]
    sent = {
        name: [block(target) for target in targets]
        for name, block in (("gate", gate_block), ("up", up_block), ("down", down_block))
    }
    moved = {(name, 0): blocks[0] for name, blocks in sent.items()}

    def begin(first, *units_sent):
        blocks = [sent[name][k] for name, k in units_sent]
        if first is not None:
            first, blocks = lax.optimization_barrier((first, blocks))
        arriving = [from_peer(block, "q", NQ, k) for block, (_, k) in zip(blocks, units_sent)]
        return first, (units_sent, arriving)

    def end(last, flight):
        units_sent, arriving = flight
        last, arriving = lax.optimization_barrier((last, arriving))
        moved.update(zip(units_sent, arriving))
        return last

    rows = keys_values.shape[0]
    _, flight = begin(None, ("gate", 1), ("up", 1), ("gate", 2))
    column = end(gather_column(keys_values, x_index), flight)
    column, flight = begin(column, ("up", 2))
    segment = end(share(column, ("y", "core"), NY * NC), flight).reshape(NCTX * rows, 2 * HD)
    attended = attend(
        queries, segment[:, :HD], segment[:, HD:], key_positions(rows), ctx_index
    )
    attended, flight = begin(attended, ("gate", 3))

    share_rows = attended.shape[0] // (NPLANE * NZ)
    attended = (
        attended.reshape(NX, NZ, NY, NC, share_rows, HD)
        .transpose(0, 2, 3, 1, 4, 5)
        .reshape(-1, HD)
    )
    partial = dot(attended, out_weight).astype(bf16).reshape(NPLANE, NZ * share_rows, model)
    partial = end(swap(partial, PLANE), flight)
    partial = jnp.sum(partial.astype(f32), axis=0).reshape(NZ, share_rows, model)
    own_group = jnp.arange(NZ)[:, None, None] == zh_index
    partial = partial + jnp.where(own_group, residual.astype(f32)[None], 0.0)
    outgoing = partial.astype(bf16).reshape(NZ * share_rows, NCTX, feat).transpose(1, 0, 2)

    routing = jnp.concatenate([expert_ids.astype(bf16), *split(gate_values)], axis=1)
    fields = routing.shape[1]
    routing = lax.dynamic_slice_in_dim(routing, ctx_index * share_rows, share_rows, 0)
    routing = jnp.pad(routing, ((0, 0), (0, HD - fields)))
    routing = jnp.where(own_group, routing[None], 0).reshape(1, NZ * share_rows, HD)
    routing = jnp.broadcast_to(routing, (NCTX,) + routing.shape[1:])
    outgoing = jnp.concatenate([outgoing, routing], axis=2)
    outgoing, flight = begin(outgoing, ("up", 3), ("down", 1), ("down", 2))
    wide = feat + HD
    outgoing = jnp.broadcast_to(
        outgoing[:, None], (NCTX, NZ, NZ * share_rows, wide)
    ).reshape(NCTX * NZ, NZ * share_rows, wide)
    arrived = swap(outgoing, CTX + ("zh",)).reshape(NCTX, NZ, NZ * share_rows, wide)
    arrived = end(arrived, flight)
    arrived = jnp.sum(arrived.astype(f32), axis=1)
    hidden = arrived[:, :, :feat].astype(bf16).reshape(-1, feat)
    routing = arrived[:, :, feat : feat + fields].reshape(-1, fields)
    choices = expert_ids.shape[1]
    token_count = expert_ids.shape[0]

    hidden = jnp.concatenate(from_peers([hidden] * NQ, "q", NQ), axis=1)
    weight_in = [
        jnp.concatenate([moved[name, k] for k in range(NQ)], axis=0) for name in ("gate", "up")
    ]
    hidden, weight_in = lax.optimization_barrier((hidden, weight_in))
    gain = jnp.concatenate(
        [
            lax.dynamic_slice_in_dim(
                norm_gain, (p_index * NQ + jnp.bitwise_xor(q_index, k)) * feat, feat, 0
            )
            for k in range(NQ)
        ]
    )

    number = jnp.arange(NPLANE, dtype=jnp.int32)
    experts = (number // (NY * NC) * NZ + zh_index) * (NY * NC) + number % (NY * NC)
    experts = experts.astype(f32)
    slots = NZ * CAP
    total_slots = NPLANE * slots
    tokens = NZ * token_count
    slot_number = jnp.arange(total_slots, dtype=jnp.int32)
    slot_group = slot_number % slots // CAP
    slot_value = (slot_number % CAP).astype(f32)
    owner = (slot_number[None, :] // slots == number[:, None]).astype(bf16)

    def slots_of(table, group, time):
        picked = table[:, :choices, None] == experts
        chosen = jnp.sum(picked.astype(f32), axis=1)
        before = (group[:, None] == group[None, :]) & (time[None, :] < time[:, None])
        slot = dot(before.astype(bf16), chosen.astype(bf16))
        return jnp.where(chosen > 0, slot, -1.0).astype(bf16), picked

    row = jnp.arange(tokens, dtype=jnp.int32)
    group = row // share_rows % NZ
    table = routing
    slot, _ = slots_of(table, group, row)
    slot = lax.dot_general(owner, slot, (((0,), (1,)), ((), ())), preferred_element_type=f32)
    selector = (slot == slot_value[:, None]) & (slot_group[:, None] == group[None, :])
    selector = selector.astype(bf16)

    group = row // token_count
    table = (
        routing.reshape(NCTX, NZ, share_rows, -1).transpose(1, 0, 2, 3).reshape(tokens, -1)
    )
    slot, picked = slots_of(table, group, row)
    taken = (dot(slot, owner) == slot_value[None, :]) & (slot_group[None, :] == group[:, None])
    combine = []
    for part in (1, 2):
        gates = table[:, part * choices : (part + 1) * choices, None]
        gates = jnp.sum(jnp.where(picked, gates, 0.0), axis=1).astype(bf16)
        combine.append(jnp.where(taken, dot(gates, owner), 0.0).astype(bf16))

    buckets = dot(selector, hidden).astype(bf16).reshape(NPLANE, -1, HD)
    buckets, flight = begin(buckets, ("down", 3))
    buffer = end(swap(buckets, PLANE), flight).reshape(total_slots, width)

    rows = total_slots // NP
    chunks = 2 * units // HD
    body = call(
        gate_up_kernel,
        (NP, chunks * rows + 16, HD),
        (buffer, gain[None]),
        weight_in,
    )
    parts = [
        lax.dynamic_index_in_dim(body, jnp.bitwise_xor(p_index, k), 0, keepdims=False)
        for k in range(NP)
    ]
    summed = add(from_peers(parts, "p", NP))
    square_sum = summed[chunks * rows] + summed[chunks * rows + 1]
    scale = lax.rsqrt(square_sum[:rows] / model + 1e-06)
    pre = summed[: chunks * rows].reshape(2, chunks // 2, rows, HD) * scale[:, None]
    activated = (jax.nn.silu(pre[0]) * pre[1]).astype(bf16)
    activated = share(activated, "p", NP)
    expert_out = call(
        down_kernel,
        (total_slots, width),
        (activated.reshape(NP, chunks // 2, rows, HD),),
        [moved["down", k] for k in range(NQ)],
    )
    returned = swap(expert_out.reshape(NPLANE, -1, HD), PLANE).reshape(total_slots, width)
    mixed = dot(combine[0], returned) + dot(combine[1], returned)
    parts = [mixed[:, k * feat : (k + 1) * feat] for k in range(NQ)]
    landed = add(from_peers(parts[:1] + [part.astype(bf16) for part in parts[1:]], "q", NQ))
    landed = landed.reshape(NZ, token_count, feat)
    passed = lax.dynamic_index_in_dim(landed, NZ - 1 - zh_index, 0, keepdims=False)
    passed = from_peer(passed.astype(bf16), "zh", NZ, 1)
    landed = lax.dynamic_index_in_dim(landed, zh_index, 0, keepdims=False) + passed.astype(f32)
    stream = hidden[:, :feat].reshape(NCTX, NZ, share_rows, feat)
    stream = lax.dynamic_index_in_dim(stream, zh_index, 1, keepdims=False)
    return (stream.reshape(token_count, feat).astype(f32) + landed).astype(bf16)


def solution(mesh):
    fine = Mesh(mesh.devices.reshape(NP, NQ, NX, NZ, NY, NC), CTX + EXP)
    in_specs = (
        P(CTX, EXP),
        P(CTX, None),
        P(CTX + EXP, None),
        P(),
        P(EXP, None),
        P(EXP, None),
        P(EXP, None),
        P(EXP, CTX, None),
        P(EXP, None, CTX),
    )
    return jax.shard_map(
        shards, mesh=fine, in_specs=in_specs, out_specs=P(EXP, CTX), check_vma=False
    )
```
